32 devices in a mesh: rep: 2 (over x), tm: 16 (over z, y, core).
Axes of the slice: x: 2, y: 2, z: 4, core: 2. Of those that a mesh axis runs over, the one named last changes fastest.
Arguments:
- exo_tokens: bfloat16 [2048, 32, 1024], P('rep', 'tm'), parts along dimension 0, may hold values from -6 to 6
- queries: bfloat16 [2048, 1024], P(('rep', 'tm')), parts along dimension 0, may hold values from -80 to 80, as said below
- key_weight: bfloat16 [1024, 1024], replicated, may hold values from -0.1875 to 0.1875
- value_weight: bfloat16 [1024, 1024], replicated, may hold values from -0.1875 to 0.1875
- out_weight: bfloat16 [1024, 1024], replicated, may hold values from -0.1875 to 0.1875
- gaze_valid: int32 [2048], P(('rep', 'tm')), parts along dimension 0, may hold values 0 or 1
- window_offset: int32 [2048], P(('rep', 'tm')), parts along dimension 0, may hold values from 0 to 16
- cotangent: bfloat16 [2048, 1024], P(('rep', 'tm')), parts along dimension 0, may hold values from -6 to 6
Outputs:
- attended: bfloat16 [2048, 1024], P(('rep', 'tm')), parts along dimension 0
- d_queries: bfloat16 [2048, 1024], P(('rep', 'tm')), parts along dimension 0
- d_key_weight: float32 [2048, 1024], P(('rep', 'tm')), parts along dimension 0
- d_value_weight: float32 [2048, 1024], P(('rep', 'tm')), parts along dimension 0
- d_out_weight: float32 [2048, 1024], P(('rep', 'tm')), parts along dimension 0
The draws below stay inside these ranges and needn't reach their ends.
There are 2 independent parts, one for each index of `rep`. The reference program is written for one: setup_inputs(seed, part) draws one part's arguments, and reference() takes and returns one part's arrays. A program takes and returns all parts, laid end to end along the dimension named above; an argument that names none is the same for every part. Nothing has to cross between parts.
Inputs may be any that keep to these rules, and one draw needn't show every extreme that they name: `queries`: ego gaze query vectors.
All inputs are finite; a program needn't handle non-finite values. No bound on the sum of `gaze_valid` on one device may be relied on, other than what follows from the above.
Results may differ from the reference program's by a relative error of at most 0.025.
The reference program's roundings to bfloat16 on the way (of `keys`, `values`, `probs_b`, `context`, `masked_grad`, `d_context` and `d_scores`) count: a program that leaves them out, or rounds other values in their place, can miss the bound.
Values may be sent and summed in bfloat16 or wider, within the bound.
A program may use at most 192 MiB of HBM per device.

```python
import jax
import jax.numpy as jnp
from jax import lax

D = 1024
H = 16
HD = 64
CAM = 4
TPF = 8
W = 16
FB = 64
FRAMES = 1024


def draw_queries(key, part):
    first_key = jax.random.fold_in(key, 0)
    return jnp.clip(jax.random.normal(first_key, (FRAMES, D), jnp.float32), -4.0, 4.0).astype(jnp.bfloat16)


def with_ends(entries, rng, smallest, top_value):
    index_at = [jax.random.randint(jax.random.fold_in(rng, axis), (), 0, length) for axis, length in enumerate(entries.shape)]
    main_axis = entries.shape.index(max(entries.shape))
    next_to = index_at[:main_axis] + [(index_at[main_axis] + 1) % entries.shape[main_axis]] + index_at[main_axis + 1:]
    return entries.at[tuple(index_at)].set(smallest).at[tuple(next_to)].set(top_value)


def raised(drawn, own_key, source, target, blocks, factor):
    owner, partner = [(jnp.arange(drawn.shape[dim]) // (drawn.shape[dim] // blocks)).reshape([-1 if axis == dim else 1 for axis in range(drawn.ndim)]) for dim in (source, target)]
    chosen = jax.random.permutation(own_key, blocks)[partner]
    strong = (owner == chosen) | (owner == (partner + blocks // 2) % blocks)
    return jnp.where(strong, factor * drawn, drawn)


def block_levels(key, shape, shards, least, high):
    gain, own = 1.0, jax.random.fold_in(key, 6)
    for axis_at, parts in shards:
        draws = jnp.exp(jax.random.uniform(jax.random.fold_in(own, axis_at), (parts,), jnp.float32, least / len(shards), high / len(shards)))
        gain = gain * jnp.repeat(draws, shape[axis_at] // parts).reshape([-1 if axis == axis_at else 1 for axis in range(len(shape))])
    return gain


def noise(rng, extent, deviation, bound, shards=(), kind=jnp.bfloat16):
    loudness = block_levels(rng, extent, shards, -0.22, 0.18) if shards else 1.0
    entries = jax.random.normal(rng, extent, jnp.float32) * deviation * loudness
    return jnp.minimum(jnp.maximum(entries, -bound), bound).astype(kind)


def heavy_noise(stream_key, dims, spread, reach, cuts, heavy, kind=jnp.bfloat16):
    values = spread * jax.random.normal(stream_key, dims, jnp.float32)
    if cuts:
        values = values * block_levels(stream_key, dims, cuts, -0.22, 0.18)
    return jnp.clip(raised(values, jax.random.fold_in(stream_key, 3), *heavy), -reach, reach).astype(kind)


def setup_inputs(seed: int = 0, part: int = 0) -> dict:
    seeds = jax.random.split(jax.random.key(seed), 9)
    own_keys = jax.random.split(jax.random.fold_in(seeds[8], part), 9)
    exo_tokens = heavy_noise(own_keys[0], (FRAMES, CAM * TPF, D), 1.0, 6.0, ((1, 16),), (1, 2, 16, 2.0))
    queries = draw_queries(jax.random.fold_in(jax.random.fold_in(seeds[8], part), 71), part)
    key_weight = noise(seeds[2], (D, D), D ** -0.5, 0.1875)
    value_weight = noise(seeds[3], (D, D), D ** -0.5, 0.1875)
    out_weight = noise(seeds[4], (D, D), D ** -0.5, 0.1875)
    gaze_valid = with_ends((jax.random.randint(own_keys[5], (FRAMES,), 0, 4) < 3).astype(jnp.int32), jax.random.fold_in(own_keys[5], 1), 0, 1)
    window_offset = with_ends(jax.random.randint(own_keys[6], (FRAMES,), 0, W + 1), jax.random.fold_in(own_keys[6], 1), 0, W).astype(jnp.int32)
    cotangent = noise(own_keys[7], (FRAMES, D), 1.0, 6.0, ((0, 16),))
    return {"exo_tokens": exo_tokens, "queries": queries, "key_weight": key_weight, "value_weight": value_weight, "out_weight": out_weight, "gaze_valid": gaze_valid, "window_offset": window_offset, "cotangent": cotangent}


def attend_block(q_rows, keys, values, grad_rows, valid_rows, offset_rows, out_weight, first, total):
    n_query = q_rows.shape[0]
    n_frames = keys.shape[0]
    n_tok = keys.shape[1]
    width = q_rows.shape[1]
    scale = HD ** -0.5
    t_abs = first + jnp.arange(n_query, dtype=jnp.int32)
    f_abs = first - W + jnp.arange(n_frames, dtype=jnp.int32)
    lower = t_abs - W + offset_rows
    upper = t_abs + offset_rows
    allow = (f_abs[None, :] >= lower[:, None]) & (f_abs[None, :] <= upper[:, None])
    allow = allow & (f_abs[None, :] >= 0) & (f_abs[None, :] < total)
    allow_keys = jnp.repeat(allow, n_tok, axis=1)
    q_heads = q_rows.reshape(n_query, H, HD).astype(jnp.float32)
    k_heads = keys.reshape(n_frames * n_tok, H, HD).astype(jnp.float32)
    v_heads = values.reshape(n_frames * n_tok, H, HD).astype(jnp.float32)
    scores = jnp.einsum("thd,khd->htk", q_heads, k_heads) * scale
    scores = jnp.where(allow_keys[None], scores, -1e30)
    top = jnp.max(scores, axis=-1, keepdims=True)
    expo = jnp.exp(scores - top)
    probs = expo / jnp.sum(expo, axis=-1, keepdims=True)
    probs_b = probs.astype(jnp.bfloat16)
    context = jnp.einsum("htk,khd->thd", probs_b.astype(jnp.float32), v_heads).reshape(n_query, width).astype(jnp.bfloat16)
    valid_col = valid_rows.astype(jnp.float32)[:, None]
    attended = (jnp.dot(context, out_weight, preferred_element_type=jnp.float32) * valid_col).astype(jnp.bfloat16)
    masked_grad = (grad_rows.astype(jnp.float32) * valid_col).astype(jnp.bfloat16)
    d_context = jnp.dot(masked_grad, out_weight.T, preferred_element_type=jnp.float32).astype(jnp.bfloat16)
    d_heads = d_context.reshape(n_query, H, HD).astype(jnp.float32)
    d_probs = jnp.einsum("thd,khd->htk", d_heads, v_heads)
    d_scores = probs * (d_probs - jnp.sum(probs * d_probs, axis=-1, keepdims=True)) * scale
    d_scores = d_scores.astype(jnp.bfloat16).astype(jnp.float32)
    d_query = jnp.einsum("htk,khd->thd", d_scores, k_heads).reshape(n_query, width).astype(jnp.bfloat16)
    key_part = jnp.einsum("htk,thd->khd", d_scores, q_heads).reshape(n_frames, n_tok, width).astype(jnp.bfloat16)
    value_part = jnp.einsum("htk,thd->khd", probs_b.astype(jnp.float32), d_heads).reshape(n_frames, n_tok, width).astype(jnp.bfloat16)
    return attended, d_query, key_part, value_part, context, masked_grad


def reference(exo_tokens, queries, key_weight, value_weight, out_weight, gaze_valid, window_offset, cotangent):
    n_tok = CAM * TPF
    flat = exo_tokens.reshape(-1, D)
    keys = jnp.dot(flat, key_weight, preferred_element_type=jnp.float32).astype(jnp.bfloat16).reshape(FRAMES, n_tok, D)
    values = jnp.dot(flat, value_weight, preferred_element_type=jnp.float32).astype(jnp.bfloat16).reshape(FRAMES, n_tok, D)
    margin = jnp.zeros((W, n_tok, D), jnp.bfloat16)
    keys_pad = jnp.concatenate([margin, keys, margin], axis=0)
    values_pad = jnp.concatenate([margin, values, margin], axis=0)
    span = FB + 2 * W

    def advance(carry, index):
        acc_key, acc_value = carry
        first = index * FB
        key_rows = lax.dynamic_slice_in_dim(keys_pad, first, span, 0)
        value_rows = lax.dynamic_slice_in_dim(values_pad, first, span, 0)
        q_rows = lax.dynamic_slice_in_dim(queries, first, FB, 0)
        grad_rows = lax.dynamic_slice_in_dim(cotangent, first, FB, 0)
        valid_rows = lax.dynamic_slice_in_dim(gaze_valid, first, FB, 0)
        offset_rows = lax.dynamic_slice_in_dim(window_offset, first, FB, 0)
        attended, d_query, key_part, value_part, context, masked_grad = attend_block(
            q_rows, key_rows, value_rows, grad_rows, valid_rows, offset_rows, out_weight, first, FRAMES)
        acc_key = lax.dynamic_update_slice_in_dim(
            acc_key, lax.dynamic_slice_in_dim(acc_key, first, span, 0) + key_part.astype(jnp.float32), first, 0)
        acc_value = lax.dynamic_update_slice_in_dim(
            acc_value, lax.dynamic_slice_in_dim(acc_value, first, span, 0) + value_part.astype(jnp.float32), first, 0)
        return (acc_key, acc_value), (attended, d_query, context, masked_grad)

    start = (jnp.zeros((FRAMES + 2 * W, n_tok, D), jnp.float32), jnp.zeros((FRAMES + 2 * W, n_tok, D), jnp.float32))
    (acc_key, acc_value), (attended, d_query, context, masked_grad) = lax.scan(
        advance, start, jnp.arange(FRAMES // FB, dtype=jnp.int32))
    attended = attended.reshape(FRAMES, D)
    d_query = d_query.reshape(FRAMES, D)
    context = context.reshape(FRAMES, D)
    masked_grad = masked_grad.reshape(FRAMES, D)
    flat_f = flat.astype(jnp.float32)
    key_sum = acc_key[W:W + FRAMES].reshape(-1, D)
    value_sum = acc_value[W:W + FRAMES].reshape(-1, D)
    d_key_weight = jnp.dot(flat_f.T, key_sum, precision=lax.Precision.HIGHEST)
    d_value_weight = jnp.dot(flat_f.T, value_sum, precision=lax.Precision.HIGHEST)
    d_out_weight = jnp.dot(context.astype(jnp.float32).T, masked_grad.astype(jnp.float32), precision=lax.Precision.HIGHEST)
    return attended, d_query, d_key_weight, d_value_weight, d_out_weight
```

```python
import functools

import jax
import jax.numpy as jnp
from jax import lax
from jax.experimental import pallas as pl
from jax.experimental.pallas import tpu as pltpu
from jax.sharding import PartitionSpec as P

HD = 64
W = 16
QB = 32
GH = 4
GW = GH * HD
LANES = GH * QB
SCALE = HD ** (-0.5)
NEG = -1e30
UNROLL = 4

NT = (((1,), (1,)), ((), ()))
TN = (((0,), (0,)), ((), ()))
NN = (((1,), (0,)), ((), ()))


def dot(a, b, dims):
    return lax.dot_general(a, b, dims, preferred_element_type=jnp.float32)


def spread(rows, head_mask):
    return jnp.concatenate([rows] * GH, axis=0) * head_mask


def fold(wide, head_mask):
    kept = jnp.where(head_mask, wide, 0.0)
    total = kept[0:QB]
    for h in range(1, GH):
        total = total + kept[h * QB : (h + 1) * QB]
    return total


def head_masks():
    row = lax.broadcasted_iota(jnp.int32, (LANES, GW), 0) // QB
    col = lax.broadcasted_iota(jnp.int32, (LANES, GW), 1) // HD
    same = row == col
    return same, jnp.where(same, 1.0, 0.0).astype(jnp.bfloat16)


def window_parts(n_tok):
    n_keys = (QB + 2 * W) * n_tok
    frame = lax.broadcasted_iota(jnp.int32, (n_keys, LANES), 0) // n_tok - W
    query = lax.broadcasted_iota(jnp.int32, (n_keys, LANES), 1) % QB
    return frame, frame - query


def allowed(b, frame, ahead, offsets, total):
    f_abs = frame + b * QB
    return (
        (ahead >= offsets - W) & (ahead <= offsets) & (f_abs >= 0) & (f_abs < total)
    )


def stats_kernel(n_tok, total, q_ref, d_ref, k_ref, v_ref, off_ref, m_ref, l_ref, s_ref):
    _, mask_b = head_masks()
    frame, ahead = window_parts(n_tok)
    n_keys = frame.shape[0]

    def step(b, carry):
        rows = pl.ds(pl.multiple_of(b * QB, QB), QB)
        keys = pl.ds(pl.multiple_of(b * QB * n_tok, QB * n_tok), n_keys)
        q4 = spread(q_ref[rows, :], mask_b)
        d4 = spread(d_ref[rows, :], mask_b)
        allow = allowed(b, frame, ahead, off_ref[pl.ds(b, 1), :], total)
        scores = jnp.where(allow, dot(k_ref[keys, :], q4, NT) * SCALE, NEG)
        top = jnp.max(scores, axis=0, keepdims=True)
        expo = jnp.exp(scores - top)
        d_probs = dot(v_ref[keys, :], d4, NT)
        m_ref[0, pl.ds(b, 1), :] = top
        l_ref[0, pl.ds(b, 1), :] = jnp.sum(expo, axis=0, keepdims=True)
        s_ref[0, pl.ds(b, 1), :] = jnp.sum(expo * d_probs, axis=0, keepdims=True)
        return carry

    lax.fori_loop(0, total // QB, step, 0, unroll=UNROLL)


def value_kernel(
    n_tok, total, q_ref, d_ref, k_ref, v_ref, off_ref, m_ref, l_ref, o_ref, g_ref, acc, ctx
):
    same, mask_b = head_masks()
    frame, ahead = window_parts(n_tok)
    n_keys = frame.shape[0]
    acc[...] = jnp.zeros_like(acc)

    def step(b, carry):
        rows = pl.ds(pl.multiple_of(b * QB, QB), QB)
        keys = pl.ds(pl.multiple_of(b * QB * n_tok, QB * n_tok), n_keys)
        q4 = spread(q_ref[rows, :], mask_b)
        d4 = spread(d_ref[rows, :], mask_b)
        allow = allowed(b, frame, ahead, off_ref[pl.ds(b, 1), :], total)
        scores = jnp.where(allow, dot(k_ref[keys, :], q4, NT) * SCALE, NEG)
        probs = jnp.exp(scores - m_ref[0, pl.ds(b, 1), :]) * l_ref[0, pl.ds(b, 1), :]
        probs_b = probs.astype(jnp.bfloat16)
        ctx[rows, :] = fold(dot(probs_b, v_ref[keys, :], TN), same)
        acc[keys, :] += dot(probs_b, d4, NN)
        return carry

    lax.fori_loop(0, total // QB, step, 0, unroll=UNROLL)
    o_ref[...] = ctx[...].T.astype(jnp.bfloat16)
    g_ref[...] = acc[...].astype(jnp.bfloat16)


def key_kernel(
    n_tok, total, q_ref, d_ref, k_ref, v_ref, off_ref, m_ref, l_ref, s_ref, dq_ref, g_ref, acc
):
    same, mask_b = head_masks()
    frame, ahead = window_parts(n_tok)
    n_keys = frame.shape[0]
    acc[...] = jnp.zeros_like(acc)

    def step(b, carry):
        rows = pl.ds(pl.multiple_of(b * QB, QB), QB)
        keys = pl.ds(pl.multiple_of(b * QB * n_tok, QB * n_tok), n_keys)
        q4 = spread(q_ref[rows, :], mask_b)
        d4 = spread(d_ref[rows, :], mask_b)
        allow = allowed(b, frame, ahead, off_ref[pl.ds(b, 1), :], total)
        k_blk = k_ref[keys, :]
        scores = jnp.where(allow, dot(k_blk, q4, NT) * SCALE, NEG)
        probs = jnp.exp(scores - m_ref[0, pl.ds(b, 1), :]) * l_ref[0, pl.ds(b, 1), :]
        d_probs = dot(v_ref[keys, :], d4, NT)
        d_scores = probs * (d_probs - s_ref[0, pl.ds(b, 1), :]) * SCALE
        d_scores = d_scores.astype(jnp.bfloat16)
        dq_ref[rows, :] = fold(dot(d_scores, k_blk, TN), same).astype(jnp.bfloat16)
        acc[keys, :] += dot(d_scores, q4, NN)
        return carry

    lax.fori_loop(0, total // QB, step, 0, unroll=UNROLL)
    g_ref[...] = acc[...].astype(jnp.bfloat16)


def attention_calls(n_tok, total, width):
    groups = width // GW
    blocks = total // QB
    key_rows = (total + 2 * W) * n_tok
    by_query = pl.BlockSpec((total, GW), lambda g: (0, g))
    by_key = pl.BlockSpec((key_rows, GW), lambda g: (0, g))
    by_offset = pl.BlockSpec((blocks, LANES), lambda g: (0, 0))
    by_stat = pl.BlockSpec((1, blocks, LANES), lambda g: (g, 0, 0))
    by_feature = pl.BlockSpec((GW, total), lambda g: (g, 0))
    stat = jax.ShapeDtypeStruct((groups, blocks, LANES), jnp.float32)
    key_like = jax.ShapeDtypeStruct((key_rows, width), jnp.bfloat16)
    key_acc = pltpu.VMEM((key_rows, GW), jnp.float32)
    params = pltpu.CompilerParams(vmem_limit_bytes=48 * 1024 * 1024)
    unit = 2 * groups * blocks * (QB + 2 * W) * n_tok * LANES * GW
    common = [by_query, by_query, by_key, by_key, by_offset]

    def cost(dots):
        return pl.CostEstimate(
            flops=4 * dots * unit, bytes_accessed=8 * key_rows * width, transcendentals=0
        )

    stats = pl.pallas_call(
        functools.partial(stats_kernel, n_tok, total),
        grid=(groups,),
        in_specs=common,
        out_specs=[by_stat] * 3,
        out_shape=[stat] * 3,
        compiler_params=params,
        cost_estimate=cost(2),
        name="softmax_stats",
    )
    value = pl.pallas_call(
        functools.partial(value_kernel, n_tok, total),
        grid=(groups,),
        in_specs=common + [by_stat] * 2,
        out_specs=[by_feature, by_key],
        out_shape=[jax.ShapeDtypeStruct((width, total), jnp.bfloat16), key_like],
        scratch_shapes=[key_acc, pltpu.VMEM((total, GW), jnp.float32)],
        compiler_params=params,
        cost_estimate=cost(3),
        name="context_and_value_part",
    )
    key = pl.pallas_call(
        functools.partial(key_kernel, n_tok, total),
        grid=(groups,),
        in_specs=common + [by_stat] * 3,
        out_specs=[by_query, by_key],
        out_shape=[jax.ShapeDtypeStruct((total, width), jnp.bfloat16), key_like],
        scratch_shapes=[key_acc],
        compiler_params=params,
        cost_estimate=cost(4),
        name="query_and_key_part",
    )
    return stats, value, key


def shards(
    exo_tokens, queries, key_weight, value_weight, out_weight, gaze_valid, window_offset, cotangent
):
    rows_here = queries.shape[0]
    width = queries.shape[1]
    total = rows_here * lax.axis_size("tm")
    n_tok = exo_tokens.shape[1]
    blocks = total // QB
    valid_col = gaze_valid.astype(jnp.float32)[:, None]
    masked_grad = (cotangent.astype(jnp.float32) * valid_col).astype(jnp.bfloat16)
    extra = jnp.broadcast_to(window_offset.astype(jnp.bfloat16)[:, None], (rows_here, 128))
    q_all = lax.all_gather(queries, "tm", axis=0, tiled=True)
    grad_all = lax.all_gather(
        jnp.concatenate([masked_grad, extra], axis=1), "tm", axis=0, tiled=True
    )
    offsets = grad_all[:, width].astype(jnp.int32).reshape(blocks, 1, QB)
    offsets = jnp.broadcast_to(offsets, (blocks, GH, QB)).reshape(blocks, LANES)
    grad_all = grad_all[:, :width]

    flat = exo_tokens.reshape(-1, width)
    flat = jnp.pad(flat, ((W * n_tok, W * n_tok), (0, 0)))
    keys = dot(flat, key_weight, NN).astype(jnp.bfloat16)
    values = dot(flat, value_weight, NN).astype(jnp.bfloat16)
    d_context = dot(grad_all, out_weight, NT).astype(jnp.bfloat16)

    stats_call, value_call, key_call = attention_calls(n_tok, total, width)
    common = (q_all, d_context, keys, values, offsets)
    top, norm, slope = stats_call(*common)
    top_all = lax.pmax(top, "tm")
    factor = jnp.exp(top - top_all)
    sums = lax.psum(jnp.stack([norm * factor, slope * factor]), "tm")
    inverse = 1.0 / sums[0]
    slope_all = sums[1] * inverse

    context_t, value_part = value_call(*common, top_all, inverse)
    context_t = lax.psum_scatter(context_t, "tm", scatter_dimension=0, tiled=True)
    value_term = dot(flat, value_part, TN).astype(jnp.bfloat16)
    d_value = lax.psum_scatter(value_term, "tm", scatter_dimension=0, tiled=True)

    d_query, key_part = key_call(*common, top_all, inverse, slope_all)
    d_query = lax.psum_scatter(d_query, "tm", scatter_dimension=0, tiled=True)
    key_term = dot(flat, key_part, TN).astype(jnp.bfloat16)
    d_key = lax.psum_scatter(key_term, "tm", scatter_dimension=0, tiled=True)

    d_out = dot(context_t, grad_all, NN)
    context = lax.all_to_all(context_t, "tm", split_axis=1, concat_axis=0, tiled=True)
    attended = (dot(context, out_weight, TN) * valid_col).astype(jnp.bfloat16)
    return (
        attended,
        d_query,
        d_key.astype(jnp.float32),
        d_value.astype(jnp.float32),
        d_out,
    )


def solution(mesh):
    in_specs = (
        P("rep", "tm", None),
        P(("rep", "tm"), None),
        P(),
        P(),
        P(),
        P(("rep", "tm")),
        P(("rep", "tm")),
        P(("rep", "tm"), None),
    )
    out_specs = (P(("rep", "tm"), None),) * 5
    return jax.shard_map(shards, mesh=mesh, in_specs=in_specs, out_specs=out_specs, check_vma=False)
```

```python
import functools
import itertools

import jax
import jax.numpy as jnp
from jax import lax
from jax.experimental import pallas as pl
from jax.experimental.pallas import tpu as pltpu
from jax.sharding import PartitionSpec as P

HD = 64
W = 16
QB = 32
GH = 4
GW = GH * HD
LANES = GH * QB
SCALE = HD ** (-0.5)
NEG = -1e30
UNROLL = 4

NT = (((1,), (1,)), ((), ()))
TN = (((0,), (0,)), ((), ()))
NN = (((1,), (0,)), ((), ()))


def dot(a, b, dims):
    return lax.dot_general(a, b, dims, preferred_element_type=jnp.float32)


def spread(rows, head_mask):
    return jnp.concatenate([rows] * GH, axis=0) * head_mask


def fold(wide, head_mask):
    kept = jnp.where(head_mask, wide, 0.0)
    total = kept[0:QB]
    for h in range(1, GH):
        total = total + kept[h * QB : (h + 1) * QB]
    return total


def head_masks():
    row = lax.broadcasted_iota(jnp.int32, (LANES, GW), 0) // QB
    col = lax.broadcasted_iota(jnp.int32, (LANES, GW), 1) // HD
    same = row == col
    return same, jnp.where(same, 1.0, 0.0).astype(jnp.bfloat16)


def window_parts(n_tok):
    n_keys = (QB + 2 * W) * n_tok
    frame = lax.broadcasted_iota(jnp.int32, (n_keys, LANES), 0) // n_tok - W
    query = lax.broadcasted_iota(jnp.int32, (n_keys, LANES), 1) % QB
    return frame, frame - query


def allowed(b, frame, ahead, offsets, total):
    f_abs = frame + b * QB
    return (
        (ahead >= offsets - W) & (ahead <= offsets) & (f_abs >= 0) & (f_abs < total)
    )


def bit_of(me, k):
    return lax.rem(me // (1 << k), 2)


def partner_of(me, k):
    return me + (1 << k) * (1 - 2 * bit_of(me, k))


def greet(others):
    barrier = pltpu.get_barrier_semaphore()
    for other in others:
        pl.semaphore_signal(
            barrier, inc=1, device_id={"tm": other}, device_id_type=pl.DeviceIdType.MESH
        )
    pl.semaphore_wait(barrier, len(others))


def remote(src, dst, send, recv, other):
    return pltpu.make_async_remote_copy(
        src_ref=src,
        dst_ref=dst,
        send_sem=send,
        recv_sem=recv,
        device_id={"tm": other},
        device_id_type=pl.DeviceIdType.MESH,
    )


def at_bits(ref, bits, chosen):
    return ref.at[tuple(chosen[k] if k in chosen else slice(None) for k in bits)]


class Gather:
    def __init__(self, me, n_bits, order, out, send, recv):
        self.me, self.order, self.out = me, order, out
        self.bits = list(range(n_bits))[::-1]
        self.send, self.recv = send, recv

    def copy(self, step):
        held = {k: bit_of(self.me, k) for k in self.order[step:]}
        part = at_bits(self.out, self.bits, held)
        other = partner_of(self.me, self.order[step])
        return remote(part, part, self.send.at[step], self.recv.at[step], other)


class Reduce:
    def __init__(self, me, n_bits, order, src, slots, send, recv):
        self.me, self.order = me, order
        self.bits = list(range(n_bits))[::-1]
        self.refs = [src] + list(slots)
        self.send, self.recv = send, recv

    def left(self, step):
        return [k for k in self.bits if k not in self.order[:step]]

    def copy(self, step):
        k = self.order[step]
        part = at_bits(self.refs[step], self.left(step), {k: 1 - bit_of(self.me, k)})
        other = partner_of(self.me, k)
        return remote(part, self.refs[step + 1], self.send.at[step], self.recv.at[step], other)

    def finish(self, step):
        self.copy(step).wait()
        k = self.order[step]
        bits = self.left(step)
        rest = [other for other in bits if other != k]
        for index in itertools.product((0, 1), repeat=len(rest)):
            chosen = dict(zip(rest, index))
            chosen[k] = bit_of(self.me, k)
            own = self.refs[step][tuple(chosen[bit] for bit in bits)]
            got = self.refs[step + 1][index]
            total = own.astype(jnp.float32) + got.astype(jnp.float32)
            self.refs[step + 1][index] = total.astype(jnp.bfloat16)


def slot_shapes(n_bits, rows, width):
    return [
        pltpu.VMEM((2,) * (n_bits - 1 - step) + (rows, width), jnp.bfloat16)
        for step in range(n_bits)
    ]


def low_first(n_bits):
    return list(range(n_bits))


def late_one(n_bits):
    return [0] + list(range(2, n_bits)) + [1]


def project_kernel(
    n_bits, chunk, q_ref, g_ref, x_ref, kw_ref, vw_ref, qo_ref, go_ref, k_ref, v_ref, send, recv
):
    me = lax.axis_index("tm")
    greet([partner_of(me, k) for k in range(n_bits)])
    orders = (list(range(1, n_bits))[::-1] + [0], [1] + list(range(2, n_bits))[::-1] + [0])
    gathers = []
    for i, (mine, out) in enumerate(((q_ref, qo_ref), (g_ref, go_ref))):
        out[tuple(bit_of(me, k) for k in range(n_bits)[::-1])] = mine[...]
        gathers.append(Gather(me, n_bits, orders[i], out, send.at[i], recv.at[i]))
    for gather in gathers:
        gather.copy(0).start()
    rows, width = x_ref.shape
    n_cols = width // GW

    def piece(j, carry):
        cols = pl.ds(pl.multiple_of(j * GW, GW), GW)

        def part(i, inner):
            here = pl.ds(pl.multiple_of(i * chunk, 16), chunk)
            x = x_ref[here, :]
            k_ref[here, cols] = dot(x, kw_ref[:, cols], NN).astype(jnp.bfloat16)
            v_ref[here, cols] = dot(x, vw_ref[:, cols], NN).astype(jnp.bfloat16)
            return inner

        lax.fori_loop(0, rows // chunk, part, 0)
        return carry

    for step in range(n_bits):
        lax.fori_loop(n_cols * step // n_bits, n_cols * (step + 1) // n_bits, piece, 0)
        for gather in gathers:
            gather.copy(step).wait()
            if step + 1 < n_bits:
                gather.copy(step + 1).start()


def place(b, per, groups, g):
    return b // per, pl.ds(lax.rem(b, per) * groups + g, 1)


def stats_kernel(
    n_tok, total, n_dev, q_ref, d_ref, k_ref, v_ref, off_ref, res_ref, mine, got, out_ref,
    send, recv, send_back, recv_back,
):
    _, mask_b = head_masks()
    frame, ahead = window_parts(n_tok)
    n_keys = frame.shape[0]
    g = pl.program_id(0)
    groups = pl.num_programs(0)
    per = total // QB // n_dev
    me = lax.axis_index("tm")

    @pl.when(g == 0)
    def _():
        greet([lax.rem(me + i, n_dev) for i in range(1, n_dev)])

    def step(b, carry):
        rows = pl.ds(pl.multiple_of(b * QB, QB), QB)
        keys = pl.ds(pl.multiple_of(b * QB * n_tok, QB * n_tok), n_keys)
        q4 = spread(q_ref[rows, :], mask_b)
        d4 = spread(d_ref[rows, :], mask_b)
        allow = allowed(b, frame, ahead, off_ref[pl.ds(b, 1), :], total)
        scores = jnp.where(allow, dot(k_ref[keys, :], q4, NT) * SCALE, NEG)
        top = jnp.max(scores, axis=0, keepdims=True)
        expo = jnp.exp(scores - top)
        d_probs = dot(v_ref[keys, :], d4, NT)
        owner, row = place(b, per, groups, g)
        mine[owner, 0, row, :] = top
        mine[owner, 1, row, :] = jnp.sum(expo, axis=0, keepdims=True)
        mine[owner, 2, row, :] = jnp.sum(expo * d_probs, axis=0, keepdims=True)
        return carry

    lax.fori_loop(0, total // QB, step, 0, unroll=UNROLL)

    def there(i):
        other = lax.rem(me + i, n_dev)
        return remote(mine.at[other], got.at[i], send.at[i], recv.at[i], other)

    def back(i):
        other = lax.rem(me + i, n_dev)
        return remote(out_ref.at[me], out_ref.at[me], send_back.at[i], recv_back.at[i], other)

    @pl.when(g == groups - 1)
    def _():
        for i in range(1, n_dev):
            there(i).start()
        got[0] = mine[me]
        for i in range(1, n_dev):
            there(i).wait()
        top = got[0, 0]
        for i in range(1, n_dev):
            top = jnp.maximum(top, got[i, 0])
        norm = jnp.zeros_like(top)
        slope = jnp.zeros_like(top)
        for i in range(n_dev):
            factor = jnp.exp(got[i, 0] - top)
            norm = norm + factor * got[i, 1]
            slope = slope + factor * got[i, 2]
        inverse = 1.0 / norm
        out_ref[me, 0] = top
        out_ref[me, 1] = inverse
        out_ref[me, 2] = slope * inverse
        for i in range(1, n_dev):
            back(i).start()
        for i in range(1, n_dev):
            back(i).wait()
        res_ref[...] = out_ref[...]


def value_kernel(
    n_tok, total, n_dev, q_ref, d_ref, k_ref, v_ref, off_ref, st_ref, o_ref, g_ref, acc, ctx
):
    same, mask_b = head_masks()
    frame, ahead = window_parts(n_tok)
    n_keys = frame.shape[0]
    g = pl.program_id(0)
    groups = pl.num_programs(0)
    per = total // QB // n_dev
    acc[...] = jnp.zeros_like(acc)

    def step(b, carry):
        rows = pl.ds(pl.multiple_of(b * QB, QB), QB)
        keys = pl.ds(pl.multiple_of(b * QB * n_tok, QB * n_tok), n_keys)
        q4 = spread(q_ref[rows, :], mask_b)
        d4 = spread(d_ref[rows, :], mask_b)
        allow = allowed(b, frame, ahead, off_ref[pl.ds(b, 1), :], total)
        scores = jnp.where(allow, dot(k_ref[keys, :], q4, NT) * SCALE, NEG)
        owner, row = place(b, per, groups, g)
        probs = jnp.exp(scores - st_ref[owner, 0, row, :]) * st_ref[owner, 1, row, :]
        probs_b = probs.astype(jnp.bfloat16)
        ctx[rows, :] = fold(dot(probs_b, v_ref[keys, :], TN), same)
        acc[keys, :] += dot(probs_b, d4, NN)
        return carry

    lax.fori_loop(0, total // QB, step, 0, unroll=UNROLL)
    o_ref[...] = ctx[...].T.astype(jnp.bfloat16)
    g_ref[...] = acc[...].astype(jnp.bfloat16)


def key_kernel(
    n_tok, total, n_dev, n_bits, q_ref, d_ref, k_ref, v_ref, off_ref, st_ref, a_ref, b_ref,
    dq_ref, g_ref, ao_ref, bo_ref, acc, *rest
):
    same, mask_b = head_masks()
    frame, ahead = window_parts(n_tok)
    n_keys = frame.shape[0]
    g = pl.program_id(0)
    groups = pl.num_programs(0)
    per = total // QB // n_dev
    acc[...] = jnp.zeros_like(acc)
    me = lax.axis_index("tm")
    sums = two_reduces(me, n_bits, (a_ref, b_ref), rest)

    @pl.when(g == 0)
    def _():
        greet([partner_of(me, k) for k in range(n_bits)])
        for one in sums:
            one.copy(0).start()

    def step(b, carry):
        rows = pl.ds(pl.multiple_of(b * QB, QB), QB)
        keys = pl.ds(pl.multiple_of(b * QB * n_tok, QB * n_tok), n_keys)
        q4 = spread(q_ref[rows, :], mask_b)
        d4 = spread(d_ref[rows, :], mask_b)
        allow = allowed(b, frame, ahead, off_ref[pl.ds(b, 1), :], total)
        k_blk = k_ref[keys, :]
        scores = jnp.where(allow, dot(k_blk, q4, NT) * SCALE, NEG)
        owner, row = place(b, per, groups, g)
        probs = jnp.exp(scores - st_ref[owner, 0, row, :]) * st_ref[owner, 1, row, :]
        d_probs = dot(v_ref[keys, :], d4, NT)
        d_scores = probs * (d_probs - st_ref[owner, 2, row, :]) * SCALE
        d_scores = d_scores.astype(jnp.bfloat16)
        dq_ref[rows, :] = fold(dot(d_scores, k_blk, TN), same).astype(jnp.bfloat16)
        acc[keys, :] += dot(d_scores, q4, NN)
        return carry

    lax.fori_loop(0, total // QB, step, 0, unroll=UNROLL)
    g_ref[...] = acc[...].astype(jnp.bfloat16)

    def advance(at):
        for one in sums:
            one.finish(at)
            if at + 1 < n_bits:
                one.copy(at + 1).start()

    n_groups = b_ref.shape[-1] // GW
    for at in range(n_groups):

        @pl.when(g == at)
        def _(at=at):
            last = at + 1 if at + 1 < n_groups else n_bits
            for now in range(at, min(last, n_bits)):
                advance(now)

    @pl.when(g == n_groups - 1)
    def _():
        ao_ref[...] = sums[0].refs[-1][...]
        bo_ref[...] = sums[1].refs[-1][...].astype(jnp.float32)


def two_reduces(me, n_bits, sources, rest):
    send, recv = rest[-2:]
    orders = (low_first(n_bits), late_one(n_bits))
    return [
        Reduce(
            me, n_bits, orders[i], sources[i], rest[i * n_bits : (i + 1) * n_bits],
            send.at[i], recv.at[i],
        )
        for i in range(2)
    ]


def reduce_kernel(n_bits, a_ref, b_ref, ao_ref, bo_ref, *rest):
    me = lax.axis_index("tm")
    sums = two_reduces(me, n_bits, (a_ref, b_ref), rest)
    greet([partner_of(me, k) for k in range(n_bits)])
    for one in sums:
        one.copy(0).start()
    for at in range(n_bits):
        for one in sums:
            one.finish(at)
            if at + 1 < n_bits:
                one.copy(at + 1).start()
    ao_ref[...] = sums[0].refs[-1][...]
    bo_ref[...] = sums[1].refs[-1][...].astype(jnp.float32)


def row_chunk(rows):
    return max(c for c in range(16, 769, 16) if rows % c == 0)


def attention_calls(n_tok, total, width, n_dev):
    n_bits = n_dev.bit_length() - 1
    groups = width // GW
    blocks = total // QB
    here = total // n_dev
    key_rows = (total + 2 * W) * n_tok
    by_query = pl.BlockSpec((total, GW), lambda g: (0, g))
    by_key = pl.BlockSpec((key_rows, GW), lambda g: (0, g))
    by_offset = pl.BlockSpec((blocks, LANES), lambda g: (0, 0))
    by_feature = pl.BlockSpec((GW, total), lambda g: (g, 0))
    whole = pl.BlockSpec(memory_space=pltpu.VMEM)
    key_like = jax.ShapeDtypeStruct((key_rows, width), jnp.bfloat16)
    key_acc = pltpu.VMEM((key_rows, GW), jnp.float32)
    stat = (n_dev, 3, blocks // n_dev * groups, LANES)
    sems = [pltpu.SemaphoreType.DMA((2, n_bits))] * 2
    limit = 56 * 1024 * 1024
    unit = 2 * groups * blocks * (QB + 2 * W) * n_tok * LANES * GW
    common = [by_query, by_query, by_key, by_key, by_offset]
    bits = (2,) * n_bits

    def shape(dims, kind=jnp.bfloat16):
        return jax.ShapeDtypeStruct(dims, kind)

    def params(number):
        return pltpu.CompilerParams(
            vmem_limit_bytes=limit, collective_id=number, has_side_effects=True
        )

    def cost(flops):
        return pl.CostEstimate(
            flops=flops, bytes_accessed=8 * key_rows * width, transcendentals=0
        )

    project = pl.pallas_call(
        functools.partial(project_kernel, n_bits, row_chunk(key_rows)),
        in_specs=[whole] * 5,
        out_specs=[whole] * 4,
        out_shape=[
            shape(bits + (here, width)), shape(bits + (here, width + 128)), key_like, key_like
        ],
        scratch_shapes=sems,
        compiler_params=params(0),
        cost_estimate=cost(4 * key_rows * width * width),
        name="gather_and_project",
    )
    stats = pl.pallas_call(
        functools.partial(stats_kernel, n_tok, total, n_dev),
        grid=(groups,),
        in_specs=common,
        out_specs=whole,
        out_shape=shape(stat, jnp.float32),
        scratch_shapes=[pltpu.VMEM(stat, jnp.float32)] * 3
        + [pltpu.SemaphoreType.DMA((n_dev,))] * 4,
        compiler_params=params(1),
        cost_estimate=cost(8 * unit),
        name="softmax_stats",
    )
    value = pl.pallas_call(
        functools.partial(value_kernel, n_tok, total, n_dev),
        grid=(groups,),
        in_specs=common + [whole],
        out_specs=[by_feature, by_key],
        out_shape=[shape((width, total)), key_like],
        scratch_shapes=[key_acc, pltpu.VMEM((total, GW), jnp.float32)],
        compiler_params=pltpu.CompilerParams(vmem_limit_bytes=limit),
        cost_estimate=cost(12 * unit),
        name="context_and_value_part",
    )
    own = width // n_dev
    key = pl.pallas_call(
        functools.partial(key_kernel, n_tok, total, n_dev, n_bits),
        grid=(groups,),
        in_specs=common + [whole] * 3,
        out_specs=[by_query, by_key, whole, whole],
        out_shape=[
            shape((total, width)), key_like, shape((own, total)), shape((own, width), jnp.float32)
        ],
        scratch_shapes=[key_acc]
        + slot_shapes(n_bits, own, total)
        + slot_shapes(n_bits, own, width)
        + sems,
        compiler_params=params(2),
        cost_estimate=cost(16 * unit),
        name="query_and_key_part",
    )
    reduce = pl.pallas_call(
        functools.partial(reduce_kernel, n_bits),
        in_specs=[whole] * 2,
        out_specs=[whole] * 2,
        out_shape=[shape((here, width)), shape((own, width), jnp.float32)],
        scratch_shapes=slot_shapes(n_bits, here, width) + slot_shapes(n_bits, own, width) + sems,
        compiler_params=params(3),
        cost_estimate=cost(0),
        name="reduce_query_and_key",
    )
    return project, stats, value, key, reduce


def shards(
    exo_tokens, queries, key_weight, value_weight, out_weight, gaze_valid, window_offset, cotangent
):
    rows_here = queries.shape[0]
    width = queries.shape[1]
    total = rows_here * lax.axis_size("tm")
    n_tok = exo_tokens.shape[1]
    blocks = total // QB
    valid_col = gaze_valid.astype(jnp.float32)[:, None]
    masked_grad = (cotangent.astype(jnp.float32) * valid_col).astype(jnp.bfloat16)
    extra = jnp.broadcast_to(window_offset.astype(jnp.bfloat16)[:, None], (rows_here, 128))
    grad_wide = jnp.concatenate([masked_grad, extra], axis=1)
    flat = exo_tokens.reshape(-1, width)
    flat = jnp.pad(flat, ((W * n_tok, W * n_tok), (0, 0)))
    n_dev = lax.axis_size("tm")
    bits = (2,) * (n_dev.bit_length() - 1)
    project, stats, value, key, reduce = attention_calls(n_tok, total, width, n_dev)
    q_all, grad_all, keys, values = project(queries, grad_wide, flat, key_weight, value_weight)
    q_all = q_all.reshape(total, width)
    grad_all = grad_all.reshape(total, -1)
    offsets = grad_all[:, width].astype(jnp.int32).reshape(blocks, 1, QB)
    offsets = jnp.broadcast_to(offsets, (blocks, GH, QB)).reshape(blocks, LANES)
    grad_all = grad_all[:, :width]
    d_context = dot(grad_all, out_weight, NT).astype(jnp.bfloat16)

    common = (q_all, d_context, keys, values, offsets)
    combined = stats(*common)
    context_t, value_part = value(*common, combined)
    value_term = dot(flat, value_part, TN).astype(jnp.bfloat16)
    own = width // n_dev
    d_query, key_part, context_t, d_value = key(
        *common,
        combined,
        context_t.reshape(bits + (own, total)),
        value_term.reshape(bits + (own, width)),
    )
    key_term = dot(flat, key_part, TN).astype(jnp.bfloat16)
    d_query, d_key = reduce(
        d_query.reshape(bits + (rows_here, width)), key_term.reshape(bits + (own, width))
    )
    d_out = dot(context_t, grad_all, NN)
    context = lax.all_to_all(context_t, "tm", split_axis=1, concat_axis=0, tiled=True)
    attended = (dot(context, out_weight, TN) * valid_col).astype(jnp.bfloat16)
    return attended, d_query, d_key, d_value, d_out


def solution(mesh):
    in_specs = (
        P("rep", "tm", None),
        P(("rep", "tm"), None),
        P(),
        P(),
        P(),
        P(("rep", "tm")),
        P(("rep", "tm")),
        P(("rep", "tm"), None),
    )
    out_specs = (P(("rep", "tm"), None),) * 5
    return jax.shard_map(shards, mesh=mesh, in_specs=in_specs, out_specs=out_specs, check_vma=False)
```

```python
import functools
import itertools

import jax
import jax.numpy as jnp
from jax import lax
from jax.experimental import pallas as pl
from jax.experimental.pallas import tpu as pltpu
from jax.sharding import PartitionSpec as P

HD = 64
W = 16
QB = 32
GH = 4
GW = GH * HD
LANES = GH * QB
SCALE = HD ** (-0.5)
NEG = -1e30
UNROLL = 4

NT = (((1,), (1,)), ((), ()))
TN = (((0,), (0,)), ((), ()))
NN = (((1,), (0,)), ((), ()))


def dot(a, b, dims):
    return lax.dot_general(a, b, dims, preferred_element_type=jnp.float32)


def spread(rows, head_mask):
    return jnp.concatenate([rows] * GH, axis=0) * head_mask


def fold(wide):
    lane = lax.broadcasted_iota(jnp.int32, (QB, 2 * HD), 1)
    tiles = []
    for h in range(0, GH, 2):
        cols = slice(h * HD, (h + 2) * HD)
        first = wide[h * QB : (h + 1) * QB, cols]
        second = wide[(h + 1) * QB : (h + 2) * QB, cols]
        tiles.append(jnp.where(lane < HD, first, second))
    return jnp.concatenate(tiles, axis=1)


def head_mask():
    row = lax.broadcasted_iota(jnp.int32, (LANES, GW), 0) // QB
    col = lax.broadcasted_iota(jnp.int32, (LANES, GW), 1) // HD
    return jnp.where(row == col, 1.0, 0.0).astype(jnp.bfloat16)


def window_parts(n_tok):
    n_keys = (QB + 2 * W) * n_tok
    frame = lax.broadcasted_iota(jnp.int32, (n_keys, LANES), 0) // n_tok - W
    query = lax.broadcasted_iota(jnp.int32, (n_keys, LANES), 1) % QB
    return frame, frame - query


def allowed(b, frame, ahead, offsets, total):
    f_abs = frame + b * QB
    return (
        (ahead >= offsets - W) & (ahead <= offsets) & (f_abs >= 0) & (f_abs < total)
    )


def bit_of(me, k):
    return lax.rem(me // (1 << k), 2)


def partner_of(me, k):
    return me + (1 << k) * (1 - 2 * bit_of(me, k))


def greet(others):
    barrier = pltpu.get_barrier_semaphore()
    for other in others:
        pl.semaphore_signal(
            barrier, inc=1, device_id={"tm": other}, device_id_type=pl.DeviceIdType.MESH
        )
    pl.semaphore_wait(barrier, len(others))


def remote(src, dst, send, recv, other):
    return pltpu.make_async_remote_copy(
        src_ref=src,
        dst_ref=dst,
        send_sem=send,
        recv_sem=recv,
        device_id={"tm": other},
        device_id_type=pl.DeviceIdType.MESH,
    )


def at_bits(ref, bits, chosen):
    return ref.at[tuple(chosen[k] if k in chosen else slice(None) for k in bits)]


class Gather:
    def __init__(self, me, n_bits, order, out, send, recv):
        self.me, self.order, self.out = me, order, out
        self.bits = list(range(n_bits))[::-1]
        self.send, self.recv = send, recv

    def copy(self, step):
        held = {k: bit_of(self.me, k) for k in self.order[step:]}
        part = at_bits(self.out, self.bits, held)
        other = partner_of(self.me, self.order[step])
        return remote(part, part, self.send.at[step], self.recv.at[step], other)


class Reduce:
    def __init__(self, me, n_bits, src, first_col, slots, send, recv):
        self.me, self.order = me, list(range(n_bits))
        self.bits = list(range(n_bits))[::-1]
        self.src, self.slots = src, slots
        self.cols = pl.ds(first_col, slots[0].shape[-1])
        self.send, self.recv = send, recv

    def left(self, step):
        return [k for k in self.bits if k not in self.order[:step]]

    def copy(self, step):
        k = self.order[step]
        index = tuple(
            1 - bit_of(self.me, k) if bit == k else slice(None) for bit in self.left(step)
        )
        if step == 0:
            part = self.src.at[index + (slice(None), self.cols)]
        else:
            part = self.slots[step - 1].at[index]
        other = partner_of(self.me, k)
        return remote(part, self.slots[step], self.send.at[step], self.recv.at[step], other)

    def finish(self, step):
        self.copy(step).wait()
        k = self.order[step]
        bits = self.left(step)
        rest = [other for other in bits if other != k]
        for index in itertools.product((0, 1), repeat=len(rest)):
            chosen = dict(zip(rest, index))
            chosen[k] = bit_of(self.me, k)
            at = tuple(chosen[bit] for bit in bits)
            if step == 0:
                own = self.src[at + (slice(None), self.cols)]
            else:
                own = self.slots[step - 1][at]
            total = own.astype(jnp.float32) + self.slots[step][index].astype(jnp.float32)
            self.slots[step][index] = total.astype(jnp.bfloat16)


class Staged:
    def __init__(self, sums, starts, n_bits):
        self.sums, self.starts, self.n_bits = sums, starts, n_bits
        self.ticks = max(starts) + n_bits

    def begin(self, at):
        for one, start in zip(self.sums, self.starts):
            if start == at:
                one.copy(0).start()

    def tick(self, at):
        for one, start in zip(self.sums, self.starts):
            step = at - start
            if 0 <= step < self.n_bits:
                one.finish(step)
                if step + 1 < self.n_bits:
                    one.copy(step + 1).start()
        self.begin(at + 1)

    def write(self, refs):
        half = len(self.sums) // 2
        for i, ref in enumerate(refs):
            for j in range(half):
                one = self.sums[i * half + j]
                ref[:, one.cols] = one.slots[-1][...].astype(ref.dtype)


def slot_shapes(n_bits, rows, width):
    return [
        pltpu.VMEM((2,) * (n_bits - 1 - step) + (rows, width), jnp.bfloat16)
        for step in range(n_bits)
    ]


def project_kernel(
    n_bits, chunk, q_ref, g_ref, x_ref, kw_ref, vw_ref, qo_ref, go_ref, k_ref, v_ref, send, recv
):
    me = lax.axis_index("tm")
    greet([partner_of(me, k) for k in range(n_bits)])
    order = list(range(n_bits))[::-1]
    gathers = []
    for i, (mine, out) in enumerate(((q_ref, qo_ref), (g_ref, go_ref))):
        out[tuple(bit_of(me, k) for k in range(n_bits)[::-1])] = mine[...]
        gathers.append(Gather(me, n_bits, order, out, send.at[i], recv.at[i]))
    gathers[0].copy(0).start()
    rows, width = x_ref.shape
    n_cols = width // GW
    pad = (k_ref.shape[0] - rows) // 2
    for ref in (k_ref, v_ref):
        ref[:pad, :] = jnp.zeros((pad, width), jnp.bfloat16)
        ref[rows + pad :, :] = jnp.zeros((pad, width), jnp.bfloat16)

    def piece(j, carry):
        cols = pl.ds(pl.multiple_of(j * GW, GW), GW)

        def part(i, inner):
            here = pl.ds(pl.multiple_of(i * chunk, 16), chunk)
            there = pl.ds(pl.multiple_of(i * chunk + pad, 16), chunk)
            x = x_ref[here, :]
            k_ref[there, cols] = dot(x, kw_ref[:, cols], NN).astype(jnp.bfloat16)
            v_ref[there, cols] = dot(x, vw_ref[:, cols], NN).astype(jnp.bfloat16)
            return inner

        lax.fori_loop(0, rows // chunk, part, 0)
        return carry

    lag = 2
    ticks = n_bits + lag
    for tick in range(ticks):
        lax.fori_loop(n_cols * tick // ticks, n_cols * (tick + 1) // ticks, piece, 0)
        for gather, start in zip(gathers, (0, lag)):
            step = tick - start
            if 0 <= step < n_bits:
                gather.copy(step).wait()
            if 0 <= step + 1 < n_bits:
                gather.copy(step + 1).start()


def place(b, per, groups, g):
    return b // per, pl.ds(lax.rem(b, per) * groups + g, 1)


def stats_kernel(
    n_tok, total, n_dev, q_ref, d_ref, k_ref, v_ref, off_ref, res_ref, mine, got, out_ref,
    send, recv, send_back, recv_back,
):
    mask_b = head_mask()
    frame, ahead = window_parts(n_tok)
    n_keys = frame.shape[0]
    g = pl.program_id(0)
    groups = pl.num_programs(0)
    per = total // QB // n_dev
    me = lax.axis_index("tm")

    @pl.when(g == 0)
    def _():
        greet([lax.rem(me + i, n_dev) for i in range(1, n_dev)])

    def step(b, carry):
        rows = pl.ds(pl.multiple_of(b * QB, QB), QB)
        keys = pl.ds(pl.multiple_of(b * QB * n_tok, QB * n_tok), n_keys)
        q4 = spread(q_ref[rows, :], mask_b)
        d4 = spread(d_ref[rows, :], mask_b)
        allow = allowed(b, frame, ahead, off_ref[pl.ds(b, 1), :], total)
        scores = jnp.where(allow, dot(k_ref[keys, :], q4, NT) * SCALE, NEG)
        top = jnp.max(scores, axis=0, keepdims=True)
        expo = jnp.exp(scores - top)
        d_probs = dot(v_ref[keys, :], d4, NT)
        owner, row = place(b, per, groups, g)
        mine[owner, 0, row, :] = top
        mine[owner, 1, row, :] = jnp.sum(expo, axis=0, keepdims=True)
        mine[owner, 2, row, :] = jnp.sum(expo * d_probs, axis=0, keepdims=True)
        return carry

    lax.fori_loop(0, total // QB, step, 0, unroll=UNROLL)

    def there(i):
        other = lax.rem(me + i, n_dev)
        return remote(mine.at[other], got.at[i], send.at[i], recv.at[i], other)

    def back(i):
        other = lax.rem(me + i, n_dev)
        return remote(out_ref.at[me], out_ref.at[me], send_back.at[i], recv_back.at[i], other)

    @pl.when(g == groups - 1)
    def _():
        for i in range(1, n_dev):
            there(i).start()
        got[0] = mine[me]
        for i in range(1, n_dev):
            there(i).wait()
        top = got[0, 0]
        for i in range(1, n_dev):
            top = jnp.maximum(top, got[i, 0])
        norm = jnp.zeros_like(top)
        slope = jnp.zeros_like(top)
        for i in range(n_dev):
            factor = jnp.exp(got[i, 0] - top)
            norm = norm + factor * got[i, 1]
            slope = slope + factor * got[i, 2]
        inverse = 1.0 / norm
        out_ref[me, 0] = top
        out_ref[me, 1] = inverse
        out_ref[me, 2] = slope * inverse
        for i in range(1, n_dev):
            back(i).start()
        for i in range(1, n_dev):
            back(i).wait()
        res_ref[...] = out_ref[...]


def value_kernel(
    n_tok, total, n_dev, q_ref, d_ref, k_ref, v_ref, off_ref, st_ref, o_ref, g_ref, acc, ctx
):
    mask_b = head_mask()
    frame, ahead = window_parts(n_tok)
    n_keys = frame.shape[0]
    ahead_rows = QB * n_tok
    pad = W * n_tok
    g = pl.program_id(0)
    groups = pl.num_programs(0)
    per = total // QB // n_dev

    def step(b, carry):
        rows = pl.ds(pl.multiple_of(b * QB, QB), QB)
        first = pl.multiple_of(b * ahead_rows, ahead_rows)
        keys = pl.ds(first, n_keys)
        q4 = spread(q_ref[rows, :], mask_b)
        d4 = spread(d_ref[rows, :], mask_b)
        allow = allowed(b, frame, ahead, off_ref[pl.ds(b, 1), :], total)
        scores = jnp.where(allow, dot(k_ref[keys, :], q4, NT) * SCALE, NEG)
        owner, row = place(b, per, groups, g)
        probs = jnp.exp(scores - st_ref[owner, 0, row, :]) * st_ref[owner, 1, row, :]
        probs_b = probs.astype(jnp.bfloat16)
        ctx[rows, :] = fold(dot(probs_b, v_ref[keys, :], TN))
        part = dot(probs_b, d4, NN)
        acc[pl.ds(first, ahead_rows), :] = (carry + part[:ahead_rows]).astype(jnp.bfloat16)
        return part[ahead_rows:]

    zero = jnp.zeros((ahead_rows, GW), jnp.float32)
    tail = lax.fori_loop(0, total // QB, step, zero, unroll=UNROLL)
    acc[total * n_tok :, :] = tail.astype(jnp.bfloat16)
    o_ref[...] = ctx[...].T.astype(jnp.bfloat16)
    g_ref[...] = acc[pad : pad + total * n_tok, :]


def key_kernel(
    n_tok, total, n_dev, n_bits, q_ref, d_ref, k_ref, v_ref, off_ref, st_ref, a_ref, b_ref,
    dq_ref, g_ref, ao_ref, bo_ref, acc, *rest
):
    mask_b = head_mask()
    frame, ahead = window_parts(n_tok)
    n_keys = frame.shape[0]
    ahead_rows = QB * n_tok
    pad = W * n_tok
    g = pl.program_id(0)
    groups = pl.num_programs(0)
    per = total // QB // n_dev
    me = lax.axis_index("tm")
    staged = Staged(four_sums(me, n_bits, (a_ref, b_ref), rest), (0, 1, 2, 3), n_bits)

    @pl.when(g == 0)
    def _():
        greet([partner_of(me, k) for k in range(n_bits)])
        staged.begin(0)

    def step(b, carry):
        rows = pl.ds(pl.multiple_of(b * QB, QB), QB)
        first = pl.multiple_of(b * ahead_rows, ahead_rows)
        keys = pl.ds(first, n_keys)
        q4 = spread(q_ref[rows, :], mask_b)
        d4 = spread(d_ref[rows, :], mask_b)
        allow = allowed(b, frame, ahead, off_ref[pl.ds(b, 1), :], total)
        k_blk = k_ref[keys, :]
        scores = jnp.where(allow, dot(k_blk, q4, NT) * SCALE, NEG)
        owner, row = place(b, per, groups, g)
        probs = jnp.exp(scores - st_ref[owner, 0, row, :]) * st_ref[owner, 1, row, :]
        d_probs = dot(v_ref[keys, :], d4, NT)
        d_scores = probs * (d_probs - st_ref[owner, 2, row, :]) * SCALE
        d_scores = d_scores.astype(jnp.bfloat16)
        dq_ref[rows, :] = fold(dot(d_scores, k_blk, TN)).astype(jnp.bfloat16)
        part = dot(d_scores, q4, NN)
        acc[pl.ds(first, ahead_rows), :] = (carry + part[:ahead_rows]).astype(jnp.bfloat16)
        return part[ahead_rows:]

    n_groups = b_ref.shape[-1] // GW
    points = 2 * n_groups
    half = total // QB // 2
    tail = jnp.zeros((ahead_rows, GW), jnp.float32)
    for side in range(2):
        tail = lax.fori_loop(side * half, (side + 1) * half, step, tail, unroll=UNROLL)
        for at in range(side, points, 2):

            @pl.when(g == at // 2)
            def _(at=at):
                last = at + 1 if at + 1 < points else staged.ticks
                for now in range(at, min(last, staged.ticks)):
                    staged.tick(now)

    acc[total * n_tok :, :] = tail.astype(jnp.bfloat16)
    g_ref[...] = acc[pad : pad + total * n_tok, :]

    @pl.when(g == n_groups - 1)
    def _():
        staged.write((ao_ref, bo_ref))


def four_sums(me, n_bits, sources, rest):
    send, recv = rest[-2:]
    sums = []
    for i in range(4):
        slots = rest[i * n_bits : (i + 1) * n_bits]
        first_col = (i % 2) * slots[0].shape[-1]
        source = sources[i // 2]
        sums.append(Reduce(me, n_bits, source, first_col, slots, send.at[i], recv.at[i]))
    return sums


def reduce_kernel(n_bits, a_ref, x_ref, g_ref, ao_ref, bo_ref, term, *rest):
    me = lax.axis_index("tm")
    staged = Staged(four_sums(me, n_bits, (a_ref, term), rest), (0, 1, 2, 4), n_bits)
    greet([partner_of(me, k) for k in range(n_bits)])
    staged.begin(0)
    width = x_ref.shape[1]
    own = term.shape[-2]
    half = width // 2
    for tick in range(staged.ticks):
        if tick < 4:
            cols = slice(tick // 2 * half, (tick // 2 + 1) * half)
            for first in range(tick % 2 * half, (tick % 2 + 1) * half, GW):
                product = dot(x_ref[:, first : first + GW], g_ref[:, cols], TN)
                product = product.astype(jnp.bfloat16)
                for i in range(GW // own):
                    owner = first // own + i
                    index = tuple((owner >> k) % 2 for k in range(n_bits)[::-1])
                    term[index + (slice(None), cols)] = product[i * own : (i + 1) * own]
        staged.tick(tick)
    staged.write((ao_ref, bo_ref))


def row_chunk(rows):
    return max(c for c in range(16, 769, 16) if rows % c == 0)


def attention_calls(n_tok, total, width, n_dev):
    n_bits = n_dev.bit_length() - 1
    groups = width // GW
    blocks = total // QB
    here = total // n_dev
    key_rows = (total + 2 * W) * n_tok
    by_query = pl.BlockSpec((total, GW), lambda g: (0, g))
    by_key = pl.BlockSpec((key_rows, GW), lambda g: (0, g))
    by_offset = pl.BlockSpec((blocks, LANES), lambda g: (0, 0))
    by_feature = pl.BlockSpec((GW, total), lambda g: (g, 0))
    whole = pl.BlockSpec(memory_space=pltpu.VMEM)
    key_like = jax.ShapeDtypeStruct((key_rows, width), jnp.bfloat16)
    part_like = jax.ShapeDtypeStruct((total * n_tok, width), jnp.bfloat16)
    by_part = pl.BlockSpec((total * n_tok, GW), lambda g: (0, g))
    key_acc = pltpu.VMEM((key_rows, GW), jnp.bfloat16)
    stat = (n_dev, 3, blocks // n_dev * groups, LANES)
    sems = [pltpu.SemaphoreType.DMA((4, n_bits))] * 2
    limit = 56 * 1024 * 1024
    unit = 2 * groups * blocks * (QB + 2 * W) * n_tok * LANES * GW
    common = [by_query, by_query, by_key, by_key, by_offset]
    bits = (2,) * n_bits

    def shape(dims, kind=jnp.bfloat16):
        return jax.ShapeDtypeStruct(dims, kind)

    def params(number):
        return pltpu.CompilerParams(
            vmem_limit_bytes=limit, collective_id=number, has_side_effects=True
        )

    def cost(flops):
        return pl.CostEstimate(
            flops=flops, bytes_accessed=8 * key_rows * width, transcendentals=0
        )

    project = pl.pallas_call(
        functools.partial(project_kernel, n_bits, row_chunk(total * n_tok)),
        in_specs=[whole] * 5,
        out_specs=[whole] * 4,
        out_shape=[
            shape(bits + (here, width)), shape(bits + (here, width + 128)), key_like, key_like
        ],
        scratch_shapes=sems,
        compiler_params=params(0),
        cost_estimate=cost(4 * key_rows * width * width),
        name="gather_and_project",
    )
    stats = pl.pallas_call(
        functools.partial(stats_kernel, n_tok, total, n_dev),
        grid=(groups,),
        in_specs=common,
        out_specs=whole,
        out_shape=shape(stat, jnp.float32),
        scratch_shapes=[pltpu.VMEM(stat, jnp.float32)] * 3
        + [pltpu.SemaphoreType.DMA((n_dev,))] * 4,
        compiler_params=params(1),
        cost_estimate=cost(8 * unit),
        name="softmax_stats",
    )
    value = pl.pallas_call(
        functools.partial(value_kernel, n_tok, total, n_dev),
        grid=(groups,),
        in_specs=common + [whole],
        out_specs=[by_feature, by_part],
        out_shape=[shape((width, total)), part_like],
        scratch_shapes=[key_acc, pltpu.VMEM((total, GW), jnp.float32)],
        compiler_params=pltpu.CompilerParams(vmem_limit_bytes=limit),
        cost_estimate=cost(12 * unit),
        name="context_and_value_part",
    )
    own = width // n_dev
    key = pl.pallas_call(
        functools.partial(key_kernel, n_tok, total, n_dev, n_bits),
        grid=(groups,),
        in_specs=common + [whole] * 3,
        out_specs=[by_query, by_part, whole, whole],
        out_shape=[
            shape((total, width)), part_like, shape((own, total)), shape((own, width), jnp.float32)
        ],
        scratch_shapes=[key_acc]
        + slot_shapes(n_bits, own, total // 2) * 2
        + slot_shapes(n_bits, own, width // 2) * 2
        + sems,
        compiler_params=params(2),
        cost_estimate=cost(16 * unit),
        name="query_and_key_part",
    )
    reduce = pl.pallas_call(
        functools.partial(reduce_kernel, n_bits),
        in_specs=[whole] * 3,
        out_specs=[whole] * 2,
        out_shape=[shape((here, width)), shape((own, width), jnp.float32)],
        scratch_shapes=[pltpu.VMEM(bits + (own, width), jnp.bfloat16)]
        + slot_shapes(n_bits, here, width // 2) * 2
        + slot_shapes(n_bits, own, width // 2) * 2
        + sems,
        compiler_params=params(3),
        cost_estimate=cost(2 * key_rows * width * width),
        name="reduce_query_and_key",
    )
    return project, stats, value, key, reduce


def shards(
    exo_tokens, queries, key_weight, value_weight, out_weight, gaze_valid, window_offset, cotangent
):
    rows_here = queries.shape[0]
    width = queries.shape[1]
    total = rows_here * lax.axis_size("tm")
    n_tok = exo_tokens.shape[1]
    blocks = total // QB
    valid_col = gaze_valid.astype(jnp.float32)[:, None]
    masked_grad = (cotangent.astype(jnp.float32) * valid_col).astype(jnp.bfloat16)
    extra = jnp.broadcast_to(window_offset.astype(jnp.bfloat16)[:, None], (rows_here, 128))
    grad_wide = jnp.concatenate([masked_grad, extra], axis=1)
    flat = exo_tokens.reshape(-1, width)
    n_dev = lax.axis_size("tm")
    bits = (2,) * (n_dev.bit_length() - 1)
    project, stats, value, key, reduce = attention_calls(n_tok, total, width, n_dev)
    q_all, grad_all, keys, values = project(queries, grad_wide, flat, key_weight, value_weight)
    q_all = q_all.reshape(total, width)
    grad_all = grad_all.reshape(total, -1)
    offsets = grad_all[:, width].astype(jnp.int32).reshape(blocks, 1, QB)
    offsets = jnp.broadcast_to(offsets, (blocks, GH, QB)).reshape(blocks, LANES)
    grad_all = grad_all[:, :width]
    d_context = dot(grad_all, out_weight, NT).astype(jnp.bfloat16)

    common = (q_all, d_context, keys, values, offsets)
    combined = stats(*common)
    context_t, value_part = value(*common, combined)
    value_term = dot(flat, value_part, TN).astype(jnp.bfloat16)
    own = width // n_dev
    d_query, key_part, context_t, d_value = key(
        *common,
        combined,
        context_t.reshape(bits + (own, total)),
        value_term.reshape(bits + (own, width)),
    )
    d_query, d_key = reduce(d_query.reshape(bits + (rows_here, width)), flat, key_part)
    d_out = dot(context_t, grad_all, NN)
    context = lax.all_to_all(context_t, "tm", split_axis=1, concat_axis=0, tiled=True)
    attended = (dot(context, out_weight, TN) * valid_col).astype(jnp.bfloat16)
    return attended, d_query, d_key, d_value, d_out


def solution(mesh):
    in_specs = (
        P("rep", "tm", None),
        P(("rep", "tm"), None),
        P(),
        P(),
        P(),
        P(("rep", "tm")),
        P(("rep", "tm")),
        P(("rep", "tm"), None),
    )
    out_specs = (P(("rep", "tm"), None),) * 5
    return jax.shard_map(shards, mesh=mesh, in_specs=in_specs, out_specs=out_specs, check_vma=False)
```

```python
import functools
import itertools

import jax
import jax.numpy as jnp
from jax import lax
from jax.experimental import pallas as pl
from jax.experimental.pallas import tpu as pltpu
from jax.sharding import PartitionSpec as P

HD = 64
W = 16
QB = 32
GH = 4
GW = GH * HD
LANES = GH * QB
SCALE = HD ** (-0.5)
NEG = -1e30
UNROLL = 4

NT = (((1,), (1,)), ((), ()))
TN = (((0,), (0,)), ((), ()))
NN = (((1,), (0,)), ((), ()))


def dot(a, b, dims):
    return lax.dot_general(a, b, dims, preferred_element_type=jnp.float32)


def spread(rows, head_mask):
    return jnp.concatenate([rows] * GH, axis=0) * head_mask


def fold(wide):
    lane = lax.broadcasted_iota(jnp.int32, (QB, 2 * HD), 1)
    tiles = []
    for h in range(0, GH, 2):
        cols = slice(h * HD, (h + 2) * HD)
        first = wide[h * QB : (h + 1) * QB, cols]
        second = wide[(h + 1) * QB : (h + 2) * QB, cols]
        tiles.append(jnp.where(lane < HD, first, second))
    return jnp.concatenate(tiles, axis=1)


def head_mask():
    row = lax.broadcasted_iota(jnp.int32, (LANES, GW), 0) // QB
    col = lax.broadcasted_iota(jnp.int32, (LANES, GW), 1) // HD
    return jnp.where(row == col, 1.0, 0.0).astype(jnp.bfloat16)


def window_parts(n_tok):
    n_keys = (QB + 2 * W) * n_tok
    frame = lax.broadcasted_iota(jnp.int32, (n_keys, LANES), 0) // n_tok - W
    query = lax.broadcasted_iota(jnp.int32, (n_keys, LANES), 1) % QB
    return frame, frame - query


def allowed(b, frame, ahead, offsets, total):
    f_abs = frame + b * QB
    return (
        (ahead >= offsets - W) & (ahead <= offsets) & (f_abs >= 0) & (f_abs < total)
    )


def bit_of(me, k):
    return lax.rem(me // (1 << k), 2)


def partner_of(me, k):
    return me + (1 << k) * (1 - 2 * bit_of(me, k))


def greet(others):
    barrier = pltpu.get_barrier_semaphore()
    for other in others:
        pl.semaphore_signal(
            barrier, inc=1, device_id={"tm": other}, device_id_type=pl.DeviceIdType.MESH
        )
    pl.semaphore_wait(barrier, len(others))


def remote(src, dst, send, recv, other):
    return pltpu.make_async_remote_copy(
        src_ref=src,
        dst_ref=dst,
        send_sem=send,
        recv_sem=recv,
        device_id={"tm": other},
        device_id_type=pl.DeviceIdType.MESH,
    )


def at_bits(ref, bits, chosen):
    return ref.at[tuple(chosen[k] if k in chosen else slice(None) for k in bits)]


class Gather:
    def __init__(self, me, n_bits, order, out, send, recv):
        self.me, self.order, self.out = me, order, out
        self.bits = list(range(n_bits))[::-1]
        self.send, self.recv = send, recv

    def copy(self, step):
        held = {k: bit_of(self.me, k) for k in self.order[step:]}
        part = at_bits(self.out, self.bits, held)
        other = partner_of(self.me, self.order[step])
        return remote(part, part, self.send.at[step], self.recv.at[step], other)


class Reduce:
    def __init__(self, me, n_bits, order, src, slots, send, recv):
        self.me, self.order = me, order
        self.bits = list(range(n_bits))[::-1]
        self.src, self.slots = src, slots
        self.send, self.recv = send, recv

    def left(self, step):
        return [k for k in self.bits if k not in self.order[:step]]

    def copy(self, step):
        k = self.order[step]
        index = tuple(
            1 - bit_of(self.me, k) if bit == k else slice(None) for bit in self.left(step)
        )
        if step == 0:
            part = self.src.at[index]
        else:
            part = self.slots[step - 1].at[index]
        other = partner_of(self.me, k)
        return remote(part, self.slots[step], self.send.at[step], self.recv.at[step], other)

    def finish(self, step):
        self.copy(step).wait()
        k = self.order[step]
        bits = self.left(step)
        rest = [other for other in bits if other != k]
        for index in itertools.product((0, 1), repeat=len(rest)):
            chosen = dict(zip(rest, index))
            chosen[k] = bit_of(self.me, k)
            at = tuple(chosen[bit] for bit in bits)
            if step == 0:
                own = self.src[at]
            else:
                own = self.slots[step - 1][at]
            total = own.astype(jnp.float32) + self.slots[step][index].astype(jnp.float32)
            self.slots[step][index] = total.astype(jnp.bfloat16)


    def advance(self, step):
        self.finish(step)
        if step + 1 < len(self.order):
            self.copy(step + 1).start()


def two_sums(me, n_bits, sources, rest):
    send, recv = rest[-2:]
    orders = (list(range(n_bits)), [0] + list(range(2, n_bits)) + [1])
    return [
        Reduce(
            me, n_bits, orders[i], sources[i], rest[i * n_bits : (i + 1) * n_bits],
            send.at[i], recv.at[i],
        )
        for i in range(2)
    ]


def slot_shapes(n_bits, rows, width):
    return [
        pltpu.VMEM((2,) * (n_bits - 1 - step) + (rows, width), jnp.bfloat16)
        for step in range(n_bits)
    ]


def project_kernel(
    n_bits, chunk, q_ref, g_ref, x_any, kw_any, vw_any, qo_ref, go_ref, k_any, v_any,
    x_ref, kw_ref, vw_ref, k_ref, v_ref, send, recv, local,
):
    me = lax.axis_index("tm")
    loads = [
        pltpu.make_async_copy(src, dst, local.at[i])
        for i, (src, dst) in enumerate(((x_any, x_ref), (kw_any, kw_ref), (vw_any, vw_ref)))
    ]
    stores = [
        pltpu.make_async_copy(src, dst, local.at[3 + i])
        for i, (src, dst) in enumerate(((k_ref, k_any), (v_ref, v_any)))
    ]
    for load in loads:
        load.start()
    greet([partner_of(me, k) for k in range(n_bits)])
    orders = (list(range(1, n_bits))[::-1] + [0], [1] + list(range(2, n_bits))[::-1] + [0])
    gathers = []
    for i, (mine, out) in enumerate(((q_ref, qo_ref), (g_ref, go_ref))):
        out[tuple(bit_of(me, k) for k in range(n_bits)[::-1])] = mine[...]
        gathers.append(Gather(me, n_bits, orders[i], out, send.at[i], recv.at[i]))
    for gather in gathers:
        gather.copy(0).start()
    rows, width = x_ref.shape
    n_cols = width // GW
    pad = (k_ref.shape[0] - rows) // 2
    for ref in (k_ref, v_ref):
        ref[:pad, :] = jnp.zeros((pad, width), jnp.bfloat16)
        ref[rows + pad :, :] = jnp.zeros((pad, width), jnp.bfloat16)

    def piece(j, carry):
        cols = pl.ds(pl.multiple_of(j * GW, GW), GW)

        def part(i, inner):
            here = pl.ds(pl.multiple_of(i * chunk, 16), chunk)
            there = pl.ds(pl.multiple_of(i * chunk + pad, 16), chunk)
            x = x_ref[here, :]
            k_ref[there, cols] = dot(x, kw_ref[:, cols], NN).astype(jnp.bfloat16)
            v_ref[there, cols] = dot(x, vw_ref[:, cols], NN).astype(jnp.bfloat16)
            return inner

        lax.fori_loop(0, rows // chunk, part, 0)
        return carry

    for load in loads:
        load.wait()
    before = n_bits - 1
    for step in range(n_bits):
        if step < before:
            lax.fori_loop(n_cols * step // before, n_cols * (step + 1) // before, piece, 0)
        if step == before:
            for store in stores:
                store.start()
        for gather in gathers:
            gather.copy(step).wait()
            if step + 1 < n_bits:
                gather.copy(step + 1).start()
    for store in stores:
        store.wait()


def place(b, per, item):
    return b // per, pl.ds(item * per + lax.rem(b, per), 1)


def stats_kernel(
    n_tok, total, n_dev, q_ref, d_ref, k_ref, v_ref, off_ref, res_ref, mine, got, out_ref,
    send, recv, send_back, recv_back,
):
    mask_b = head_mask()
    frame, ahead = window_parts(n_tok)
    n_keys = frame.shape[0]
    g = pl.program_id(0)
    groups = pl.num_programs(0)
    per = total // QB // n_dev
    me = lax.axis_index("tm")

    @pl.when(g == 0)
    def _():
        greet([lax.rem(me + i, n_dev) for i in range(1, n_dev)])

    mine[g] = jnp.zeros(mine.shape[1:], jnp.float32)

    def step(b, carry):
        rows = pl.ds(pl.multiple_of(b * QB, QB), QB)
        keys = pl.ds(pl.multiple_of(b * QB * n_tok, QB * n_tok), n_keys)
        q4 = spread(q_ref[rows, :], mask_b)
        d4 = spread(d_ref[rows, :], mask_b)
        allow = allowed(b, frame, ahead, off_ref[pl.ds(b, 1), :], total)
        scores = jnp.where(allow, dot(k_ref[keys, :], q4, NT) * SCALE, NEG)
        top = jnp.max(scores, axis=0, keepdims=True)
        expo = jnp.exp(scores - top)
        d_probs = dot(v_ref[keys, :], d4, NT)
        sums = (top, jnp.sum(expo, axis=0, keepdims=True))
        sums += (jnp.sum(expo * d_probs, axis=0, keepdims=True),)
        for item, row in enumerate(sums):
            owner, at = place(b, per, item)
            mine[g, owner, at, :] = row
        return carry

    lax.fori_loop(0, total // QB, step, 0, unroll=UNROLL)

    def there(h, i):
        other = lax.rem(me + i, n_dev)
        return remote(mine.at[h, other], got.at[h, i], send.at[h, i], recv.at[h, i], other)

    def back(h, i):
        other = lax.rem(me + i, n_dev)
        own = out_ref.at[h, me]
        return remote(own, own, send_back.at[h, i], recv_back.at[h, i], other)

    def combine(h):
        got[h, 0] = mine[h, me]
        for i in range(1, n_dev):
            there(h, i).wait()
        top = got[h, 0, :per]
        for i in range(1, n_dev):
            top = jnp.maximum(top, got[h, i, :per])
        norm = jnp.zeros_like(top)
        slope = jnp.zeros_like(top)
        for i in range(n_dev):
            factor = jnp.exp(got[h, i, :per] - top)
            norm = norm + factor * got[h, i, per : 2 * per]
            slope = slope + factor * got[h, i, 2 * per : 3 * per]
        inverse = 1.0 / norm
        out_ref[h, me, :per] = top
        out_ref[h, me, per : 2 * per] = inverse
        out_ref[h, me, 2 * per : 3 * per] = slope * inverse
        for i in range(1, n_dev):
            back(h, i).start()

    for i in range(1, n_dev):
        there(g, i).start()

    @pl.when(g > 0)
    def _():
        combine(g - 1)

    @pl.when(g == groups - 1)
    def _():
        combine(g)

        def settle(h, carry):
            for i in range(1, n_dev):
                back(h, i).wait()
            return carry

        lax.fori_loop(0, groups, settle, 0)
        res_ref[...] = out_ref[...]


def value_kernel(
    n_tok, total, n_dev, q_ref, d_ref, k_ref, v_ref, off_ref, st_ref, o_ref, g_ref, acc, ctx
):
    mask_b = head_mask()
    frame, ahead = window_parts(n_tok)
    n_keys = frame.shape[0]
    ahead_rows = QB * n_tok
    pad = W * n_tok
    g = pl.program_id(0)
    groups = pl.num_programs(0)
    per = total // QB // n_dev

    def step(b, carry):
        rows = pl.ds(pl.multiple_of(b * QB, QB), QB)
        first = pl.multiple_of(b * ahead_rows, ahead_rows)
        keys = pl.ds(first, n_keys)
        q4 = spread(q_ref[rows, :], mask_b)
        d4 = spread(d_ref[rows, :], mask_b)
        allow = allowed(b, frame, ahead, off_ref[pl.ds(b, 1), :], total)
        scores = jnp.where(allow, dot(k_ref[keys, :], q4, NT) * SCALE, NEG)
        owner, top = place(b, per, 0)
        inverse = place(b, per, 1)[1]
        probs = jnp.exp(scores - st_ref[g, owner, top, :]) * st_ref[g, owner, inverse, :]
        probs_b = probs.astype(jnp.bfloat16)
        ctx[rows, :] = fold(dot(probs_b, v_ref[keys, :], TN))
        part = dot(probs_b, d4, NN)
        acc[pl.ds(first, ahead_rows), :] = (carry + part[:ahead_rows]).astype(jnp.bfloat16)
        return part[ahead_rows:]

    zero = jnp.zeros((ahead_rows, GW), jnp.float32)
    tail = lax.fori_loop(0, total // QB, step, zero, unroll=UNROLL)
    acc[total * n_tok :, :] = tail.astype(jnp.bfloat16)
    o_ref[...] = ctx[...].T.astype(jnp.bfloat16)
    g_ref[...] = acc[pad : pad + total * n_tok, :]


def key_kernel(
    n_tok, total, n_dev, n_bits, q_ref, d_ref, k_ref, v_ref, off_ref, st_ref, a_ref, b_ref,
    dq_ref, g_ref, ao_ref, bo_ref, acc, *rest
):
    mask_b = head_mask()
    frame, ahead = window_parts(n_tok)
    n_keys = frame.shape[0]
    ahead_rows = QB * n_tok
    pad = W * n_tok
    g = pl.program_id(0)
    groups = pl.num_programs(0)
    per = total // QB // n_dev
    me = lax.axis_index("tm")
    sums = two_sums(me, n_bits, (a_ref, b_ref), rest)

    @pl.when(g == 0)
    def _():
        greet([partner_of(me, k) for k in range(n_bits)])
        for one in sums:
            one.copy(0).start()

    def step(b, carry):
        rows = pl.ds(pl.multiple_of(b * QB, QB), QB)
        first = pl.multiple_of(b * ahead_rows, ahead_rows)
        keys = pl.ds(first, n_keys)
        q4 = spread(q_ref[rows, :], mask_b)
        d4 = spread(d_ref[rows, :], mask_b)
        allow = allowed(b, frame, ahead, off_ref[pl.ds(b, 1), :], total)
        k_blk = k_ref[keys, :]
        scores = jnp.where(allow, dot(k_blk, q4, NT) * SCALE, NEG)
        owner, top = place(b, per, 0)
        inverse = place(b, per, 1)[1]
        probs = jnp.exp(scores - st_ref[g, owner, top, :]) * st_ref[g, owner, inverse, :]
        d_probs = dot(v_ref[keys, :], d4, NT)
        d_scores = probs * (d_probs - st_ref[g, owner, place(b, per, 2)[1], :]) * SCALE
        d_scores = d_scores.astype(jnp.bfloat16)
        dq_ref[rows, :] = fold(dot(d_scores, k_blk, TN)).astype(jnp.bfloat16)
        part = dot(d_scores, q4, NN)
        acc[pl.ds(first, ahead_rows), :] = (carry + part[:ahead_rows]).astype(jnp.bfloat16)
        return part[ahead_rows:]

    zero = jnp.zeros((ahead_rows, GW), jnp.float32)
    tail = lax.fori_loop(0, total // QB, step, zero, unroll=UNROLL)
    acc[total * n_tok :, :] = tail.astype(jnp.bfloat16)
    g_ref[...] = acc[pad : pad + total * n_tok, :]

    n_groups = b_ref.shape[-1] // GW
    for at in range(n_groups):

        @pl.when(g == at)
        def _(at=at):
            last = at + 1 if at + 1 < n_groups else n_bits
            for now in range(at, min(last, n_bits)):
                for one in sums:
                    one.advance(now)

    @pl.when(g == n_groups - 1)
    def _():
        ao_ref[...] = sums[0].slots[-1][...]
        bo_ref[...] = sums[1].slots[-1][...].astype(jnp.float32)


def reduce_kernel(n_bits, a_ref, x_ref, g_ref, ao_ref, bo_ref, term, *rest):
    me = lax.axis_index("tm")
    first, second = two_sums(me, n_bits, (a_ref, term), rest)
    greet([partner_of(me, k) for k in range(n_bits)])
    first.copy(0).start()
    width = x_ref.shape[1]
    own = term.shape[-2]
    for col in range(0, width, GW):
        product = dot(x_ref[:, col : col + GW], g_ref[...], TN).astype(jnp.bfloat16)
        for i in range(GW // own):
            owner = col // own + i
            index = tuple((owner >> k) % 2 for k in range(n_bits)[::-1])
            term[index] = product[i * own : (i + 1) * own]
        if col == GW:
            first.advance(0)
    second.copy(0).start()
    second.advance(0)
    first.advance(1)
    for step in range(2, n_bits):
        first.advance(step)
        second.advance(step - 1)
    second.advance(n_bits - 1)
    ao_ref[...] = first.slots[-1][...]
    bo_ref[...] = second.slots[-1][...].astype(jnp.float32)


def row_chunk(rows):
    return max(c for c in range(16, 769, 16) if rows % c == 0)


def attention_calls(n_tok, total, width, n_dev):
    n_bits = n_dev.bit_length() - 1
    groups = width // GW
    blocks = total // QB
    here = total // n_dev
    key_rows = (total + 2 * W) * n_tok
    by_query = pl.BlockSpec((total, GW), lambda g: (0, g))
    by_key = pl.BlockSpec((key_rows, GW), lambda g: (0, g))
    by_offset = pl.BlockSpec((blocks, LANES), lambda g: (0, 0))
    by_feature = pl.BlockSpec((GW, total), lambda g: (g, 0))
    whole = pl.BlockSpec(memory_space=pltpu.VMEM)
    key_like = jax.ShapeDtypeStruct((key_rows, width), jnp.bfloat16)
    part_like = jax.ShapeDtypeStruct((total * n_tok, width), jnp.bfloat16)
    by_part = pl.BlockSpec((total * n_tok, GW), lambda g: (0, g))
    key_acc = pltpu.VMEM((key_rows, GW), jnp.bfloat16)
    stat = (groups, n_dev, -(-3 * (blocks // n_dev) // 8) * 8, LANES)
    sems = [pltpu.SemaphoreType.DMA((2, n_bits))] * 2
    anywhere = pl.BlockSpec(memory_space=pl.ANY)
    limit = 56 * 1024 * 1024
    unit = 2 * groups * blocks * (QB + 2 * W) * n_tok * LANES * GW
    common = [by_query, by_query, by_key, by_key, by_offset]
    bits = (2,) * n_bits

    def shape(dims, kind=jnp.bfloat16):
        return jax.ShapeDtypeStruct(dims, kind)

    def params(number):
        return pltpu.CompilerParams(
            vmem_limit_bytes=limit, collective_id=number, has_side_effects=True
        )

    def cost(flops):
        return pl.CostEstimate(
            flops=flops, bytes_accessed=8 * key_rows * width, transcendentals=0
        )

    project = pl.pallas_call(
        functools.partial(project_kernel, n_bits, row_chunk(total * n_tok)),
        in_specs=[whole] * 2 + [anywhere] * 3,
        out_specs=[whole] * 2 + [anywhere] * 2,
        out_shape=[
            shape(bits + (here, width)), shape(bits + (here, width + 128)), key_like, key_like
        ],
        scratch_shapes=[pltpu.VMEM((total * n_tok, width), jnp.bfloat16)]
        + [pltpu.VMEM((width, width), jnp.bfloat16)] * 2
        + [pltpu.VMEM((key_rows, width), jnp.bfloat16)] * 2
        + sems
        + [pltpu.SemaphoreType.DMA((5,))],
        compiler_params=params(0),
        cost_estimate=cost(4 * key_rows * width * width),
        name="gather_and_project",
    )
    stats = pl.pallas_call(
        functools.partial(stats_kernel, n_tok, total, n_dev),
        grid=(groups,),
        in_specs=common,
        out_specs=whole,
        out_shape=shape(stat, jnp.float32),
        scratch_shapes=[pltpu.VMEM(stat, jnp.float32)] * 3
        + [pltpu.SemaphoreType.DMA((groups, n_dev))] * 4,
        compiler_params=params(1),
        cost_estimate=cost(8 * unit),
        name="softmax_stats",
    )
    value = pl.pallas_call(
        functools.partial(value_kernel, n_tok, total, n_dev),
        grid=(groups,),
        in_specs=common + [whole],
        out_specs=[by_feature, by_part],
        out_shape=[shape((width, total)), part_like],
        scratch_shapes=[key_acc, pltpu.VMEM((total, GW), jnp.float32)],
        compiler_params=pltpu.CompilerParams(vmem_limit_bytes=limit),
        cost_estimate=cost(12 * unit),
        name="context_and_value_part",
    )
    own = width // n_dev
    key = pl.pallas_call(
        functools.partial(key_kernel, n_tok, total, n_dev, n_bits),
        grid=(groups,),
        in_specs=common + [whole] * 3,
        out_specs=[by_query, by_part, whole, whole],
        out_shape=[
            shape((total, width)), part_like, shape((own, total)), shape((own, width), jnp.float32)
        ],
        scratch_shapes=[key_acc]
        + slot_shapes(n_bits, own, total)
        + slot_shapes(n_bits, own, width)
        + sems,
        compiler_params=params(2),
        cost_estimate=cost(16 * unit),
        name="query_and_key_part",
    )
    reduce = pl.pallas_call(
        functools.partial(reduce_kernel, n_bits),
        in_specs=[whole] * 3,
        out_specs=[whole] * 2,
        out_shape=[shape((here, width)), shape((own, width), jnp.float32)],
        scratch_shapes=[pltpu.VMEM(bits + (own, width), jnp.bfloat16)]
        + slot_shapes(n_bits, here, width)
        + slot_shapes(n_bits, own, width)
        + sems,
        compiler_params=params(3),
        cost_estimate=cost(2 * key_rows * width * width),
        name="reduce_query_and_key",
    )
    return project, stats, value, key, reduce


def shards(
    exo_tokens, queries, key_weight, value_weight, out_weight, gaze_valid, window_offset, cotangent
):
    rows_here = queries.shape[0]
    width = queries.shape[1]
    total = rows_here * lax.axis_size("tm")
    n_tok = exo_tokens.shape[1]
    blocks = total // QB
    valid_col = gaze_valid.astype(jnp.float32)[:, None]
    masked_grad = (cotangent.astype(jnp.float32) * valid_col).astype(jnp.bfloat16)
    extra = jnp.broadcast_to(window_offset.astype(jnp.bfloat16)[:, None], (rows_here, 128))
    grad_wide = jnp.concatenate([masked_grad, extra], axis=1)
    flat = exo_tokens.reshape(-1, width)
    n_dev = lax.axis_size("tm")
    bits = (2,) * (n_dev.bit_length() - 1)
    project, stats, value, key, reduce = attention_calls(n_tok, total, width, n_dev)
    q_all, grad_all, keys, values = project(queries, grad_wide, flat, key_weight, value_weight)
    q_all = q_all.reshape(total, width)
    grad_all = grad_all.reshape(total, -1)
    offsets = grad_all[:, width].astype(jnp.int32).reshape(blocks, 1, QB)
    offsets = jnp.broadcast_to(offsets, (blocks, GH, QB)).reshape(blocks, LANES)
    grad_all = grad_all[:, :width]
    d_context = dot(grad_all, out_weight, NT).astype(jnp.bfloat16)

    common = (q_all, d_context, keys, values, offsets)
    combined = stats(*common)
    context_t, value_part = value(*common, combined)
    value_term = dot(flat, value_part, TN).astype(jnp.bfloat16)
    own = width // n_dev
    d_query, key_part, context_t, d_value = key(
        *common,
        combined,
        context_t.reshape(bits + (own, total)),
        value_term.reshape(bits + (own, width)),
    )
    d_query, d_key = reduce(d_query.reshape(bits + (rows_here, width)), flat, key_part)
    d_out = dot(context_t, grad_all, NN)
    context = lax.all_to_all(context_t, "tm", split_axis=1, concat_axis=0, tiled=True)
    attended = (dot(context, out_weight, TN) * valid_col).astype(jnp.bfloat16)
    return attended, d_query, d_key, d_value, d_out


def solution(mesh):
    in_specs = (
        P("rep", "tm", None),
        P(("rep", "tm"), None),
        P(),
        P(),
        P(),
        P(("rep", "tm")),
        P(("rep", "tm")),
        P(("rep", "tm"), None),
    )
    out_specs = (P(("rep", "tm"), None),) * 5
    return jax.shard_map(shards, mesh=mesh, in_specs=in_specs, out_specs=out_specs, check_vma=False)
```

```python
import functools
import itertools

import jax
import jax.numpy as jnp
from jax import lax
from jax.experimental import pallas as pl
from jax.experimental.pallas import tpu as pltpu
from jax.sharding import PartitionSpec as P

HD = 64
W = 16
QB = 32
GH = 4
GW = GH * HD
LANES = GH * QB
SCALE = HD ** (-0.5)
NEG = -1e30
UNROLL = 4

NT = (((1,), (1,)), ((), ()))
TN = (((0,), (0,)), ((), ()))
NN = (((1,), (0,)), ((), ()))


def dot(a, b, dims):
    return lax.dot_general(a, b, dims, preferred_element_type=jnp.float32)


def spread(rows, head_mask):
    return jnp.concatenate([rows] * GH, axis=0) * head_mask


def fold(wide):
    lane = lax.broadcasted_iota(jnp.int32, (QB, 2 * HD), 1)
    tiles = []
    for h in range(0, GH, 2):
        cols = slice(h * HD, (h + 2) * HD)
        first = wide[h * QB : (h + 1) * QB, cols]
        second = wide[(h + 1) * QB : (h + 2) * QB, cols]
        tiles.append(jnp.where(lane < HD, first, second))
    return jnp.concatenate(tiles, axis=1)


def head_mask():
    row = lax.broadcasted_iota(jnp.int32, (LANES, GW), 0) // QB
    col = lax.broadcasted_iota(jnp.int32, (LANES, GW), 1) // HD
    return jnp.where(row == col, 1.0, 0.0).astype(jnp.bfloat16)


def window_parts(n_tok):
    n_keys = (QB + 2 * W) * n_tok
    frame = lax.broadcasted_iota(jnp.int32, (n_keys, LANES), 0) // n_tok - W
    query = lax.broadcasted_iota(jnp.int32, (n_keys, LANES), 1) % QB
    return frame, frame - query


def allowed(b, frame, ahead, offsets, total):
    f_abs = frame + b * QB
    return (
        (ahead >= offsets - W) & (ahead <= offsets) & (f_abs >= 0) & (f_abs < total)
    )


def bit_of(me, k):
    return lax.rem(me // (1 << k), 2)


def partner_of(me, k):
    return me + (1 << k) * (1 - 2 * bit_of(me, k))


def greet(others):
    barrier = pltpu.get_barrier_semaphore()
    for other in others:
        pl.semaphore_signal(
            barrier, inc=1, device_id={"tm": other}, device_id_type=pl.DeviceIdType.MESH
        )
    pl.semaphore_wait(barrier, len(others))


def remote(src, dst, send, recv, other):
    return pltpu.make_async_remote_copy(
        src_ref=src,
        dst_ref=dst,
        send_sem=send,
        recv_sem=recv,
        device_id={"tm": other},
        device_id_type=pl.DeviceIdType.MESH,
    )


def at_bits(ref, bits, chosen):
    return ref.at[tuple(chosen[k] if k in chosen else slice(None) for k in bits)]


class Gather:
    def __init__(self, me, n_bits, order, out, send, recv):
        self.me, self.order, self.out = me, order, out
        self.bits = list(range(n_bits))[::-1]
        self.send, self.recv = send, recv

    def copy(self, step):
        held = {k: bit_of(self.me, k) for k in self.order[step:]}
        part = at_bits(self.out, self.bits, held)
        other = partner_of(self.me, self.order[step])
        return remote(part, part, self.send.at[step], self.recv.at[step], other)


class Reduce:
    def __init__(self, me, n_bits, order, src, first_col, slots, send, recv):
        self.me, self.order = me, order
        self.cols = pl.ds(first_col, slots[0].shape[-1])
        self.bits = list(range(n_bits))[::-1]
        self.src, self.slots = src, slots
        self.send, self.recv = send, recv

    def left(self, step):
        return [k for k in self.bits if k not in self.order[:step]]

    def copy(self, step):
        k = self.order[step]
        index = tuple(
            1 - bit_of(self.me, k) if bit == k else slice(None) for bit in self.left(step)
        )
        if step == 0:
            part = self.src.at[index + (slice(None), self.cols)]
        else:
            part = self.slots[step - 1].at[index]
        other = partner_of(self.me, k)
        return remote(part, self.slots[step], self.send.at[step], self.recv.at[step], other)

    def finish(self, step):
        self.copy(step).wait()
        k = self.order[step]
        bits = self.left(step)
        rest = [other for other in bits if other != k]
        for index in itertools.product((0, 1), repeat=len(rest)):
            chosen = dict(zip(rest, index))
            chosen[k] = bit_of(self.me, k)
            at = tuple(chosen[bit] for bit in bits)
            if step == 0:
                own = self.src[at + (slice(None), self.cols)]
            else:
                own = self.slots[step - 1][at]
            total = own.astype(jnp.float32) + self.slots[step][index].astype(jnp.float32)
            self.slots[step][index] = total.astype(jnp.bfloat16)


    def advance(self, step):
        self.finish(step)
        if step + 1 < len(self.order):
            self.copy(step + 1).start()


def two_sums(me, n_bits, sources, rest):
    send, recv = rest[-2:]
    orders = (list(range(n_bits)), [0] + list(range(2, n_bits)) + [1])
    return [
        Reduce(
            me, n_bits, orders[i], sources[i], 0, rest[i * n_bits : (i + 1) * n_bits],
            send.at[i], recv.at[i],
        )
        for i in range(2)
    ]


def slot_shapes(n_bits, rows, width):
    return [
        pltpu.VMEM((2,) * (n_bits - 1 - step) + (rows, width), jnp.bfloat16)
        for step in range(n_bits)
    ]


def project_kernel(
    n_bits, chunk, q_ref, g_ref, x_any, kw_any, vw_any, qo_ref, go_ref, k_any, v_any,
    x_ref, kw_ref, vw_ref, k_ref, v_ref, send, recv, local,
):
    me = lax.axis_index("tm")
    loads = [
        pltpu.make_async_copy(src, dst, local.at[i])
        for i, (src, dst) in enumerate(((x_any, x_ref), (kw_any, kw_ref), (vw_any, vw_ref)))
    ]
    stores = [
        pltpu.make_async_copy(src, dst, local.at[3 + i])
        for i, (src, dst) in enumerate(((k_ref, k_any), (v_ref, v_any)))
    ]
    for load in loads:
        load.start()
    greet([partner_of(me, k) for k in range(n_bits)])
    orders = (list(range(1, n_bits))[::-1] + [0], [1] + list(range(2, n_bits))[::-1] + [0])
    gathers = []
    for i, (mine, out) in enumerate(((q_ref, qo_ref), (g_ref, go_ref))):
        out[tuple(bit_of(me, k) for k in range(n_bits)[::-1])] = mine[...]
        gathers.append(Gather(me, n_bits, orders[i], out, send.at[i], recv.at[i]))
    for gather in gathers:
        gather.copy(0).start()
    rows, width = x_ref.shape
    n_cols = width // GW
    pad = (k_ref.shape[0] - rows) // 2
    for ref in (k_ref, v_ref):
        ref[:pad, :] = jnp.zeros((pad, width), jnp.bfloat16)
        ref[rows + pad :, :] = jnp.zeros((pad, width), jnp.bfloat16)

    def piece(j, carry):
        cols = pl.ds(pl.multiple_of(j * GW, GW), GW)

        def part(i, inner):
            here = pl.ds(pl.multiple_of(i * chunk, 16), chunk)
            there = pl.ds(pl.multiple_of(i * chunk + pad, 16), chunk)
            x = x_ref[here, :]
            k_ref[there, cols] = dot(x, kw_ref[:, cols], NN).astype(jnp.bfloat16)
            v_ref[there, cols] = dot(x, vw_ref[:, cols], NN).astype(jnp.bfloat16)
            return inner

        lax.fori_loop(0, rows // chunk, part, 0)
        return carry

    for load in loads:
        load.wait()
    before = n_bits - 1
    for step in range(n_bits):
        if step < before:
            lax.fori_loop(n_cols * step // before, n_cols * (step + 1) // before, piece, 0)
        if step == before:
            for store in stores:
                store.start()
        for gather in gathers:
            gather.copy(step).wait()
            if step + 1 < n_bits:
                gather.copy(step + 1).start()
    for store in stores:
        store.wait()


def place(b, per, item):
    return b // per, pl.ds(item * per + lax.rem(b, per), 1)


def stats_kernel(
    n_tok, total, n_dev, q_ref, d_ref, k_ref, v_ref, off_ref, res_ref, mine, got, out_ref,
    send, recv, send_back, recv_back,
):
    mask_b = head_mask()
    frame, ahead = window_parts(n_tok)
    n_keys = frame.shape[0]
    g = pl.program_id(0)
    groups = pl.num_programs(0)
    per = total // QB // n_dev
    me = lax.axis_index("tm")

    @pl.when(g == 0)
    def _():
        greet([lax.rem(me + i, n_dev) for i in range(1, n_dev)])

    mine[g] = jnp.zeros(mine.shape[1:], jnp.float32)

    def step(b, carry):
        rows = pl.ds(pl.multiple_of(b * QB, QB), QB)
        keys = pl.ds(pl.multiple_of(b * QB * n_tok, QB * n_tok), n_keys)
        q4 = spread(q_ref[rows, :], mask_b)
        d4 = spread(d_ref[rows, :], mask_b)
        allow = allowed(b, frame, ahead, off_ref[pl.ds(b, 1), :], total)
        scores = jnp.where(allow, dot(k_ref[keys, :], q4, NT) * SCALE, NEG)
        top = jnp.max(scores, axis=0, keepdims=True)
        expo = jnp.exp(scores - top)
        d_probs = dot(v_ref[keys, :], d4, NT)
        sums = (top, jnp.sum(expo, axis=0, keepdims=True))
        sums += (jnp.sum(expo * d_probs, axis=0, keepdims=True),)
        for item, row in enumerate(sums):
            owner, at = place(b, per, item)
            mine[g, owner, at, :] = row
        return carry

    lax.fori_loop(0, total // QB, step, 0, unroll=UNROLL)

    def there(h, i):
        other = lax.rem(me + i, n_dev)
        return remote(mine.at[h, other], got.at[h, i], send.at[h, i], recv.at[h, i], other)

    def back(h, i):
        other = lax.rem(me + i, n_dev)
        own = out_ref.at[h, me]
        return remote(own, own, send_back.at[h, i], recv_back.at[h, i], other)

    def combine(h):
        got[h, 0] = mine[h, me]
        for i in range(1, n_dev):
            there(h, i).wait()
        top = got[h, 0, :per]
        for i in range(1, n_dev):
            top = jnp.maximum(top, got[h, i, :per])
        norm = jnp.zeros_like(top)
        slope = jnp.zeros_like(top)
        for i in range(n_dev):
            factor = jnp.exp(got[h, i, :per] - top)
            norm = norm + factor * got[h, i, per : 2 * per]
            slope = slope + factor * got[h, i, 2 * per : 3 * per]
        inverse = 1.0 / norm
        out_ref[h, me, :per] = top
        out_ref[h, me, per : 2 * per] = inverse
        out_ref[h, me, 2 * per : 3 * per] = slope * inverse
        for i in range(1, n_dev):
            back(h, i).start()

    for i in range(1, n_dev):
        there(g, i).start()

    @pl.when(g > 0)
    def _():
        combine(g - 1)

    @pl.when(g == groups - 1)
    def _():
        combine(g)

        def settle(h, carry):
            for i in range(1, n_dev):
                back(h, i).wait()
            return carry

        lax.fori_loop(0, groups, settle, 0)
        res_ref[...] = out_ref[...]


def value_kernel(
    n_tok, total, n_dev, q_ref, d_ref, k_ref, v_ref, off_ref, st_ref, o_ref, g_ref, acc, ctx
):
    mask_b = head_mask()
    frame, ahead = window_parts(n_tok)
    n_keys = frame.shape[0]
    ahead_rows = QB * n_tok
    pad = W * n_tok
    g = pl.program_id(0)
    groups = pl.num_programs(0)
    per = total // QB // n_dev

    def step(b, carry):
        rows = pl.ds(pl.multiple_of(b * QB, QB), QB)
        first = pl.multiple_of(b * ahead_rows, ahead_rows)
        keys = pl.ds(first, n_keys)
        q4 = spread(q_ref[rows, :], mask_b)
        d4 = spread(d_ref[rows, :], mask_b)
        allow = allowed(b, frame, ahead, off_ref[pl.ds(b, 1), :], total)
        scores = jnp.where(allow, dot(k_ref[keys, :], q4, NT) * SCALE, NEG)
        owner, top = place(b, per, 0)
        inverse = place(b, per, 1)[1]
        probs = jnp.exp(scores - st_ref[g, owner, top, :]) * st_ref[g, owner, inverse, :]
        probs_b = probs.astype(jnp.bfloat16)
        ctx[rows, :] = fold(dot(probs_b, v_ref[keys, :], TN))
        part = dot(probs_b, d4, NN)
        acc[pl.ds(first, ahead_rows), :] = (carry + part[:ahead_rows]).astype(jnp.bfloat16)
        return part[ahead_rows:]

    zero = jnp.zeros((ahead_rows, GW), jnp.float32)
    tail = lax.fori_loop(0, total // QB, step, zero, unroll=UNROLL)
    acc[total * n_tok :, :] = tail.astype(jnp.bfloat16)
    o_ref[...] = ctx[...].T.astype(jnp.bfloat16)
    g_ref[...] = acc[pad : pad + total * n_tok, :]


def key_kernel(
    n_tok, total, n_dev, n_bits, q_ref, d_ref, k_ref, v_ref, off_ref, st_ref, a_ref, b_ref,
    dq_ref, g_ref, ao_ref, bo_ref, acc, *rest
):
    mask_b = head_mask()
    frame, ahead = window_parts(n_tok)
    n_keys = frame.shape[0]
    ahead_rows = QB * n_tok
    pad = W * n_tok
    g = pl.program_id(0)
    groups = pl.num_programs(0)
    per = total // QB // n_dev
    me = lax.axis_index("tm")
    sums = two_sums(me, n_bits, (a_ref, b_ref), rest)

    @pl.when(g == 0)
    def _():
        greet([partner_of(me, k) for k in range(n_bits)])
        for one in sums:
            one.copy(0).start()

    def step(b, carry):
        rows = pl.ds(pl.multiple_of(b * QB, QB), QB)
        first = pl.multiple_of(b * ahead_rows, ahead_rows)
        keys = pl.ds(first, n_keys)
        q4 = spread(q_ref[rows, :], mask_b)
        d4 = spread(d_ref[rows, :], mask_b)
        allow = allowed(b, frame, ahead, off_ref[pl.ds(b, 1), :], total)
        k_blk = k_ref[keys, :]
        scores = jnp.where(allow, dot(k_blk, q4, NT) * SCALE, NEG)
        owner, top = place(b, per, 0)
        inverse = place(b, per, 1)[1]
        probs = jnp.exp(scores - st_ref[g, owner, top, :]) * st_ref[g, owner, inverse, :]
        d_probs = dot(v_ref[keys, :], d4, NT)
        d_scores = probs * (d_probs - st_ref[g, owner, place(b, per, 2)[1], :]) * SCALE
        d_scores = d_scores.astype(jnp.bfloat16)
        dq_ref[rows, :] = fold(dot(d_scores, k_blk, TN)).astype(jnp.bfloat16)
        part = dot(d_scores, q4, NN)
        acc[pl.ds(first, ahead_rows), :] = (carry + part[:ahead_rows]).astype(jnp.bfloat16)
        return part[ahead_rows:]

    zero = jnp.zeros((ahead_rows, GW), jnp.float32)
    tail = lax.fori_loop(0, total // QB, step, zero, unroll=UNROLL)
    acc[total * n_tok :, :] = tail.astype(jnp.bfloat16)
    g_ref[...] = acc[pad : pad + total * n_tok, :]

    n_groups = b_ref.shape[-1] // GW
    for at in range(n_groups):

        @pl.when(g == at)
        def _(at=at):
            last = at + 1 if at + 1 < n_groups else n_bits
            for now in range(at, min(last, n_bits)):
                for one in sums:
                    one.advance(now)

    @pl.when(g == n_groups - 1)
    def _():
        ao_ref[...] = sums[0].slots[-1][...]
        bo_ref[...] = sums[1].slots[-1][...].astype(jnp.float32)


class Staged:
    def __init__(self, sums, starts, n_bits):
        self.sums, self.starts, self.n_bits = sums, starts, n_bits
        self.ticks = max(starts) + n_bits

    def begin(self, at):
        for one, start in zip(self.sums, self.starts):
            if start == at:
                one.copy(0).start()

    def tick(self, at):
        for one, start in zip(self.sums, self.starts):
            if 0 <= at - start < self.n_bits:
                one.advance(at - start)
        self.begin(at + 1)

    def write(self, refs):
        half = len(self.sums) // 2
        for i, ref in enumerate(refs):
            for one in self.sums[i * half : (i + 1) * half]:
                ref[:, one.cols] = one.slots[-1][...].astype(ref.dtype)


def four_sums(me, n_bits, sources, rest):
    send, recv = rest[-2:]
    order = list(range(n_bits))
    sums = []
    for i in range(4):
        slots = rest[i * n_bits : (i + 1) * n_bits]
        first_col = (i % 2) * slots[0].shape[-1]
        source = sources[i // 2]
        sums.append(Reduce(me, n_bits, order, source, first_col, slots, send.at[i], recv.at[i]))
    return sums


def reduce_kernel(n_bits, a_ref, x_ref, g_ref, ao_ref, bo_ref, term, *rest):
    me = lax.axis_index("tm")
    staged = Staged(four_sums(me, n_bits, (a_ref, term), rest), (0, 1, 2, 3), n_bits)
    greet([partner_of(me, k) for k in range(n_bits)])
    staged.begin(0)
    width = x_ref.shape[1]
    own = term.shape[-2]
    half = width // 2
    pieces = ((0, 1), (2,), (3,))
    for tick in range(staged.ticks):
        for piece in pieces[tick] if tick < len(pieces) else ():
            cols = slice(piece // 2 * half, (piece // 2 + 1) * half)
            for first in range(piece % 2 * half, (piece % 2 + 1) * half, GW):
                product = dot(x_ref[:, first : first + GW], g_ref[:, cols], TN)
                product = product.astype(jnp.bfloat16)
                for i in range(GW // own):
                    owner = first // own + i
                    index = tuple((owner >> k) % 2 for k in range(n_bits)[::-1])
                    term[index + (slice(None), cols)] = product[i * own : (i + 1) * own]
        staged.tick(tick)
    staged.write((ao_ref, bo_ref))


def row_chunk(rows):
    return max(c for c in range(16, 769, 16) if rows % c == 0)


def attention_calls(n_tok, total, width, n_dev):
    n_bits = n_dev.bit_length() - 1
    groups = width // GW
    blocks = total // QB
    here = total // n_dev
    key_rows = (total + 2 * W) * n_tok
    by_query = pl.BlockSpec((total, GW), lambda g: (0, g))
    by_key = pl.BlockSpec((key_rows, GW), lambda g: (0, g))
    by_offset = pl.BlockSpec((blocks, LANES), lambda g: (0, 0))
    by_feature = pl.BlockSpec((GW, total), lambda g: (g, 0))
    whole = pl.BlockSpec(memory_space=pltpu.VMEM)
    key_like = jax.ShapeDtypeStruct((key_rows, width), jnp.bfloat16)
    part_like = jax.ShapeDtypeStruct((total * n_tok, width), jnp.bfloat16)
    by_part = pl.BlockSpec((total * n_tok, GW), lambda g: (0, g))
    key_acc = pltpu.VMEM((key_rows, GW), jnp.bfloat16)
    stat = (groups, n_dev, -(-3 * (blocks // n_dev) // 8) * 8, LANES)
    sems = [pltpu.SemaphoreType.DMA((2, n_bits))] * 2
    anywhere = pl.BlockSpec(memory_space=pl.ANY)
    limit = 56 * 1024 * 1024
    unit = 2 * groups * blocks * (QB + 2 * W) * n_tok * LANES * GW
    common = [by_query, by_query, by_key, by_key, by_offset]
    bits = (2,) * n_bits

    def shape(dims, kind=jnp.bfloat16):
        return jax.ShapeDtypeStruct(dims, kind)

    def params(number):
        return pltpu.CompilerParams(
            vmem_limit_bytes=limit, collective_id=number, has_side_effects=True
        )

    def cost(flops):
        return pl.CostEstimate(
            flops=flops, bytes_accessed=8 * key_rows * width, transcendentals=0
        )

    project = pl.pallas_call(
        functools.partial(project_kernel, n_bits, row_chunk(total * n_tok)),
        in_specs=[whole] * 2 + [anywhere] * 3,
        out_specs=[whole] * 2 + [anywhere] * 2,
        out_shape=[
            shape(bits + (here, width)), shape(bits + (here, width + 128)), key_like, key_like
        ],
        scratch_shapes=[pltpu.VMEM((total * n_tok, width), jnp.bfloat16)]
        + [pltpu.VMEM((width, width), jnp.bfloat16)] * 2
        + [pltpu.VMEM((key_rows, width), jnp.bfloat16)] * 2
        + sems
        + [pltpu.SemaphoreType.DMA((5,))],
        compiler_params=params(0),
        cost_estimate=cost(4 * key_rows * width * width),
        name="gather_and_project",
    )
    stats = pl.pallas_call(
        functools.partial(stats_kernel, n_tok, total, n_dev),
        grid=(groups,),
        in_specs=common,
        out_specs=whole,
        out_shape=shape(stat, jnp.float32),
        scratch_shapes=[pltpu.VMEM(stat, jnp.float32)] * 3
        + [pltpu.SemaphoreType.DMA((groups, n_dev))] * 4,
        compiler_params=params(1),
        cost_estimate=cost(8 * unit),
        name="softmax_stats",
    )
    value = pl.pallas_call(
        functools.partial(value_kernel, n_tok, total, n_dev),
        grid=(groups,),
        in_specs=common + [whole],
        out_specs=[by_feature, by_part],
        out_shape=[shape((width, total)), part_like],
        scratch_shapes=[key_acc, pltpu.VMEM((total, GW), jnp.float32)],
        compiler_params=pltpu.CompilerParams(vmem_limit_bytes=limit),
        cost_estimate=cost(12 * unit),
        name="context_and_value_part",
    )
    own = width // n_dev
    key = pl.pallas_call(
        functools.partial(key_kernel, n_tok, total, n_dev, n_bits),
        grid=(groups,),
        in_specs=common + [whole] * 3,
        out_specs=[by_query, by_part, whole, whole],
        out_shape=[
            shape((total, width)), part_like, shape((own, total)), shape((own, width), jnp.float32)
        ],
        scratch_shapes=[key_acc]
        + slot_shapes(n_bits, own, total)
        + slot_shapes(n_bits, own, width)
        + sems,
        compiler_params=params(2),
        cost_estimate=cost(16 * unit),
        name="query_and_key_part",
    )
    reduce = pl.pallas_call(
        functools.partial(reduce_kernel, n_bits),
        in_specs=[whole] * 3,
        out_specs=[whole] * 2,
        out_shape=[shape((here, width)), shape((own, width), jnp.float32)],
        scratch_shapes=[pltpu.VMEM(bits + (own, width), jnp.bfloat16)]
        + slot_shapes(n_bits, here, width // 2) * 2
        + slot_shapes(n_bits, own, width // 2) * 2
        + [pltpu.SemaphoreType.DMA((4, n_bits))] * 2,
        compiler_params=params(3),
        cost_estimate=cost(2 * key_rows * width * width),
        name="reduce_query_and_key",
    )
    return project, stats, value, key, reduce


def shards(
    exo_tokens, queries, key_weight, value_weight, out_weight, gaze_valid, window_offset, cotangent
):
    rows_here = queries.shape[0]
    width = queries.shape[1]
    total = rows_here * lax.axis_size("tm")
    n_tok = exo_tokens.shape[1]
    blocks = total // QB
    valid_col = gaze_valid.astype(jnp.float32)[:, None]
    masked_grad = (cotangent.astype(jnp.float32) * valid_col).astype(jnp.bfloat16)
    extra = jnp.broadcast_to(window_offset.astype(jnp.bfloat16)[:, None], (rows_here, 128))
    grad_wide = jnp.concatenate([masked_grad, extra], axis=1)
    flat = exo_tokens.reshape(-1, width)
    n_dev = lax.axis_size("tm")
    bits = (2,) * (n_dev.bit_length() - 1)
    project, stats, value, key, reduce = attention_calls(n_tok, total, width, n_dev)
    q_all, grad_all, keys, values = project(queries, grad_wide, flat, key_weight, value_weight)
    q_all = q_all.reshape(total, width)
    grad_all = grad_all.reshape(total, -1)
    offsets = grad_all[:, width].astype(jnp.int32).reshape(blocks, 1, QB)
    offsets = jnp.broadcast_to(offsets, (blocks, GH, QB)).reshape(blocks, LANES)
    grad_all = grad_all[:, :width]
    d_context = dot(grad_all, out_weight, NT).astype(jnp.bfloat16)

    common = (q_all, d_context, keys, values, offsets)
    combined = stats(*common)
    context_t, value_part = value(*common, combined)
    value_term = dot(flat, value_part, TN).astype(jnp.bfloat16)
    own = width // n_dev
    d_query, key_part, context_t, d_value = key(
        *common,
        combined,
        context_t.reshape(bits + (own, total)),
        value_term.reshape(bits + (own, width)),
    )
    d_query, d_key = reduce(d_query.reshape(bits + (rows_here, width)), flat, key_part)
    d_out = dot(context_t, grad_all, NN)
    context = lax.all_to_all(context_t, "tm", split_axis=1, concat_axis=0, tiled=True)
    attended = (dot(context, out_weight, TN) * valid_col).astype(jnp.bfloat16)
    return attended, d_query, d_key, d_value, d_out


def solution(mesh):
    in_specs = (
        P("rep", "tm", None),
        P(("rep", "tm"), None),
        P(),
        P(),
        P(),
        P(("rep", "tm")),
        P(("rep", "tm")),
        P(("rep", "tm"), None),
    )
    out_specs = (P(("rep", "tm"), None),) * 5
    return jax.shard_map(shards, mesh=mesh, in_specs=in_specs, out_specs=out_specs, check_vma=False)
```
